128 devices in a mesh: dp: 8 (over z, core), fsdp: 16 (over y, x).
Axes of the slice: x: 4, y: 4, z: 4, core: 2. Of those that a mesh axis runs over, the one named last changes fastest.
Arguments:
- entry_embeddings: bfloat16 [8, 1024, 4, 512], P('dp', 'fsdp'), may hold values from -6 to 6
- norm_scales: bfloat16 [2, 3, 512], P(None, None, ('dp', 'fsdp')), may hold values from 0.5 to 1.5
- triple_entry_matrix: bfloat16 [2, 2, 512, 1536], P(None, None, ('dp', 'fsdp')), may hold values from -0.25 to 0.25
- mixing_exit_matrix: bfloat16 [2, 2, 512, 512], P(None, None, ('dp', 'fsdp')), may hold values from -0.75 to 0.75
- exit_bias: bfloat16 [2, 2, 512], P(None, None, ('dp', 'fsdp')), may hold values from -4 to 4
- expanding_matrix: bfloat16 [2, 512, 2048], P(None, ('dp', 'fsdp')), may hold values from -0.25 to 0.25
- former_dense_bias: bfloat16 [2, 2048], P(None, ('dp', 'fsdp')), may hold values from -6 to 6
- contracting_matrix: bfloat16 [2, 2048, 512], P(None, ('dp', 'fsdp')), may hold values from -0.125 to 0.125
- latter_dense_bias: bfloat16 [2, 512], P(None, ('dp', 'fsdp')), may hold values from -4 to 4
- row_presence_indicator: int32 [8, 1024], P('dp'), may hold values from 0 to 1, as said below
- problem_column_number: int32 [8], P('dp'), may hold values from 1 to 4
- loss_gradient: bfloat16 [8, 1024, 4, 512], P('dp', 'fsdp'), may hold values from -6 to 6
Outputs:
- activations: float32 [8, 1024, 4, 512], P('dp', 'fsdp')
- delta_tokens: float32 [8, 1024, 4, 512], P('dp', 'fsdp')
- delta_gains: float32 [2, 3, 512], P(None, None, ('dp', 'fsdp'))
- delta_heads: float32 [2, 2, 512, 1536], P(None, None, ('dp', 'fsdp'))
- delta_merge: float32 [2, 2, 512, 512], P(None, None, ('dp', 'fsdp'))
- delta_offsets: float32 [2, 2, 512], P(None, None, ('dp', 'fsdp'))
- delta_inner: float32 [2, 512, 2048], P(None, ('dp', 'fsdp'))
- delta_thresholds: float32 [2, 2048], P(None, ('dp', 'fsdp'))
- delta_outer: float32 [2, 2048, 512], P(None, ('dp', 'fsdp'))
- delta_baselines: float32 [2, 512], P(None, ('dp', 'fsdp'))
The draws below stay inside these ranges and needn't reach their ends.
Inputs may be any that keep to these rules, and one draw needn't show every extreme that they name: `row_presence_indicator`: the first and the last of the 1024 sample slots of every task are real. Feature slots with index problem_column_number or more are padding.
All inputs are finite; a program needn't handle non-finite values.
Results may differ from the reference program's by a relative error of at most 0.033.
Values may be sent and summed in bfloat16 or wider, within the bound.
A program may use at most 192 MiB of HBM per device.

```python
import math
from functools import partial
import jax
import jax.numpy as jnp
from jax import lax

EMBED_DIMENSION = 512
HEADS = 8
HEAD_DIM = 64
FF = 2048
BLOCK_TOTAL = 2
FEAT = 4
TASKS = 8
SAMPLES = 1024


def draw_row_presence_indicator(key, part):
    key = jax.random.fold_in(key, 7)
    rate_key, roll_key = jax.random.split(key)
    rates = jax.random.randint(rate_key, (TASKS, 1), 10, 98)
    rolls = jax.random.randint(roll_key, (TASKS, SAMPLES), 0, 100)
    marks = (rolls < rates).astype(jnp.int32)
    place = jnp.arange(SAMPLES, dtype=jnp.int32)[None, :]
    ends = (place == 0) | (place == SAMPLES - 1)
    return jnp.where(ends, 1, marks).astype(jnp.int32)


def with_ends(array, rng, least, top_value):
    longest = array.shape.index(max(array.shape))
    spots = []
    for shift in (0, 1):
        where = [jax.random.randint(jax.random.fold_in(rng, axis), (), 0, length) for axis, length in enumerate(array.shape)]
        where[longest] = (where[longest] + shift) % array.shape[longest]
        spots.append(tuple(where))
    return array.at[spots[0]].set(least).at[spots[1]].set(top_value)


def shard_levels(rng, shape, cuts, smallest, high):
    def one(dim, shards_of):
        draws = jax.random.uniform(jax.random.fold_in(jax.random.fold_in(rng, 6), dim), (shards_of,), jnp.float32, smallest / len(cuts), high / len(cuts))
        return jnp.repeat(jnp.exp(draws), shape[dim] // shards_of).reshape((-1,) + (1,) * (len(shape) - dim - 1))

    level = one(*cuts[0])
    for cut in cuts[1:]:
        level = level * one(*cut)
    return level


def scatter_about(stream_key, extent, deviation, most, shards=(), held_as=jnp.bfloat16):
    level = shard_levels(stream_key, extent, shards, -0.22, 0.18) if shards else 1.0
    values = jax.random.normal(stream_key, extent, jnp.float32) * deviation * level
    return jnp.minimum(jnp.maximum(values, -most), most).astype(held_as)


def setup_inputs(seed: int = 0) -> dict:
    streams_of = jax.random.split(jax.random.key(seed), 13)
    entry_embeddings = scatter_about(streams_of[0], (TASKS, SAMPLES, FEAT, EMBED_DIMENSION), 1.0, 6.0, ((0, 8), (1, 16)))
    norm_scales = jnp.clip(1.0 + 0.1 * jax.random.normal(streams_of[1], (BLOCK_TOTAL, 3, EMBED_DIMENSION), jnp.float32), 0.5, 1.5).astype(jnp.bfloat16)
    triple_entry_matrix = scatter_about(streams_of[2], (BLOCK_TOTAL, 2, EMBED_DIMENSION, 3 * EMBED_DIMENSION), EMBED_DIMENSION ** -0.5, 0.25, ((2, 128),))
    mixing_exit_matrix = scatter_about(streams_of[3], (BLOCK_TOTAL, 2, EMBED_DIMENSION, EMBED_DIMENSION), (EMBED_DIMENSION // 8) ** -0.5, 0.75, ((2, 128),))
    exit_bias = scatter_about(streams_of[4], (BLOCK_TOTAL, 2, EMBED_DIMENSION), 0.3, 4.0, ((2, 128),))
    expanding_matrix = scatter_about(streams_of[5], (BLOCK_TOTAL, EMBED_DIMENSION, FF), EMBED_DIMENSION ** -0.5, 0.25, ((1, 128),))
    former_dense_bias = scatter_about(streams_of[6], (BLOCK_TOTAL, FF), 0.5, 6.0, ((1, 128),))
    contracting_matrix = scatter_about(streams_of[7], (BLOCK_TOTAL, FF, EMBED_DIMENSION), FF ** -0.5, 0.125, ((1, 128),))
    latter_dense_bias = scatter_about(streams_of[8], (BLOCK_TOTAL, EMBED_DIMENSION), 0.3, 4.0, ((1, 128),))
    row_presence_indicator = draw_row_presence_indicator(jax.random.fold_in(streams_of[12], 71), 0)
    problem_column_number = with_ends(jax.random.randint(streams_of[10], (TASKS,), 1, FEAT + 1), jax.random.fold_in(streams_of[10], 1), 1, FEAT).astype(jnp.int32)
    loss_gradient = scatter_about(streams_of[11], (TASKS, SAMPLES, FEAT, EMBED_DIMENSION), 1.0, 6.0, ((0, 8), (1, 16)))
    return {"entry_embeddings": entry_embeddings, "norm_scales": norm_scales, "triple_entry_matrix": triple_entry_matrix, "mixing_exit_matrix": mixing_exit_matrix, "exit_bias": exit_bias, "expanding_matrix": expanding_matrix, "former_dense_bias": former_dense_bias, "contracting_matrix": contracting_matrix, "latter_dense_bias": latter_dense_bias, "row_presence_indicator": row_presence_indicator, "problem_column_number": problem_column_number, "loss_gradient": loss_gradient}


@jax.custom_vjp
def low(v):
    return lax.optimization_barrier(v.astype(jnp.bfloat16)).astype(jnp.float32)

@jax.custom_vjp
def summed_gradient_pass(v):
    return v

def low_keep(v):
    return (low(v), None)

def low_pass(kept, grad):
    return (grad,)

def back_keep(v):
    return (v, None)

def back_low(kept, grad):
    return (low(grad),)
low.defvjp(low_keep, low_pass)
summed_gradient_pass.defvjp(back_keep, back_low)
EPS = 1e-05
EXACT_ARITHMETIC = lax.Precision.HIGHEST

def layer_norm(rows, gain):
    mean = lax.optimization_barrier(jnp.mean(rows, axis=-1, keepdims=True))
    centred = rows - mean
    spread = lax.optimization_barrier(jnp.mean(centred * centred, axis=-1, keepdims=True))
    return centred * lax.rsqrt(spread + EPS) * gain

def attention(rows, weight, combine_heads, offset, key_ok):
    width = rows.shape[-1]
    packed = summed_gradient_pass(low(jnp.einsum('bld,de->ble', rows, weight, precision=EXACT_ARITHMETIC)))
    shape = rows.shape[:2] + (HEADS, HEAD_DIM)
    query = packed[..., :width].reshape(shape)
    keys = packed[..., width:2 * width].reshape(shape)
    values = packed[..., 2 * width:].reshape(shape)
    scale = 1.0 / math.sqrt(HEAD_DIM)
    scores = summed_gradient_pass(jnp.einsum('bihc,bjhc->bhij', query, keys, precision=EXACT_ARITHMETIC) * scale)
    scores = jnp.where(key_ok[:, None, None, :], scores, -1e+30)
    probs = low(jax.nn.softmax(scores, axis=-1))
    mixed = summed_gradient_pass(low(jnp.einsum('bhij,bjhc->bihc', probs, values, precision=EXACT_ARITHMETIC))).reshape(rows.shape)
    return summed_gradient_pass(jnp.einsum('bld,de->ble', mixed, combine_heads, precision=EXACT_ARITHMETIC) + offset)

def task_forward(item, network_parameters):
    rows, marks, count = item
    norm_scales, split_into_heads, combine_heads, exit_bias, expand_dense, former_dense_bias, contract_dense, latter_dense_bias = network_parameters
    sample_ok = marks > 0
    feature_ok = jnp.arange(FEAT, dtype=jnp.int32) < count
    running_representation = rows
    for apply_block in range(BLOCK_TOTAL):
        normalized_input = low(layer_norm(running_representation, norm_scales[apply_block, 0]))
        sample_keys = jnp.broadcast_to(sample_ok[None, :], (FEAT, SAMPLES))
        branch = attention(jnp.swapaxes(normalized_input, 0, 1), split_into_heads[apply_block, 0], combine_heads[apply_block, 0], exit_bias[apply_block, 0], sample_keys)
        running_representation = running_representation + jnp.swapaxes(branch, 0, 1)
        normalized_input = low(layer_norm(running_representation, norm_scales[apply_block, 1]))
        feature_keys = jnp.broadcast_to(feature_ok[None, :], (SAMPLES, FEAT))
        running_representation = running_representation + attention(normalized_input, split_into_heads[apply_block, 1], combine_heads[apply_block, 1], exit_bias[apply_block, 1], feature_keys)
        normalized_input = low(layer_norm(running_representation, norm_scales[apply_block, 2]))
        pre = summed_gradient_pass(jnp.einsum('sfd,de->sfe', normalized_input, expand_dense[apply_block], precision=EXACT_ARITHMETIC) + former_dense_bias[apply_block])
        nonlinear_map = low(jax.nn.gelu(pre, approximate=True))
        running_representation = running_representation + summed_gradient_pass(jnp.einsum('ufz,zq->ufq', nonlinear_map, contract_dense[apply_block], precision=EXACT_ARITHMETIC) + latter_dense_bias[apply_block])
    valid = sample_ok[:, None] & feature_ok[None, :]
    return jnp.where(valid[:, :, None], running_representation, jnp.zeros_like(running_representation))

def reference(entry_embeddings, norm_scales, triple_entry_matrix, mixing_exit_matrix, exit_bias, expanding_matrix, former_dense_bias, contracting_matrix, latter_dense_bias, row_presence_indicator, problem_column_number, loss_gradient):
    network_parameters = tuple((block_parameters.astype(jnp.float32) for block_parameters in (norm_scales, triple_entry_matrix, mixing_exit_matrix, exit_bias, expanding_matrix, former_dense_bias, contracting_matrix, latter_dense_bias)))
    rows = entry_embeddings.astype(jnp.float32)

    def forward(rows, network_parameters):
        step = jax.checkpoint(partial(task_forward, network_parameters=network_parameters))
        return lax.map(step, (rows, row_presence_indicator, problem_column_number))
    activations, pullback = jax.vjp(forward, rows, network_parameters)
    delta_rows, deltas = pullback(loss_gradient.astype(jnp.float32))
    return (activations, delta_rows, deltas[0], deltas[1], deltas[2], deltas[3], deltas[4], deltas[5], deltas[6], deltas[7])
```

```python
import functools

import jax
import jax.numpy as jnp
from jax import lax
from jax.experimental import pallas as pl
from jax.experimental.pallas import tpu as pltpu
from jax.sharding import PartitionSpec as P

EPS = 1e-05
NEG = -1e30
F32 = jnp.float32
BF16 = jnp.bfloat16
MESH = pl.DeviceIdType.MESH
LAYERS = 2
TOK = 256
DIM = 512
VECS = 10
SCALE = 0.125

QKV = (0, 512)
OUT = (384, 896)
INNER = 1024
OUTER = 1536

AG_ORDERS = ("xyz", "yzx", "zxy")
AG_GROUPS = (
    (0, ((0, 128), (128, 256), (256, 384))),
    (0, ((384, 1024), (1024, 1536), (1536, 2048))),
    (1, ((0, 640), (640, 1280), (1280, 2048))),
)
RS_ORDERS = ("zyx", "xzy", "yxz")
RS_GROUPS = (
    ((1024, 1280), (1280, 1664), (1664, 2048)),
    ((512, 768), (768, 896), (896, 1024)),
    ((0, 128), (128, 384), (384, 512)),
)


def dot(a, b):
    return jnp.dot(a, b, preferred_element_type=F32)


def dot_nt(a, b):
    return lax.dot_general(a, b, (((1,), (1,)), ((), ())), preferred_element_type=F32)


def turned(a):
    return a.astype(F32).T.astype(BF16)


def colsum(a):
    return jnp.sum(a, axis=0, keepdims=True)


def lane(shape):
    return lax.broadcasted_iota(jnp.int32, shape, len(shape) - 1)


def kernel(
    x_ref,
    seed_ref,
    blocks_ref,
    outer_ref,
    vec_ref,
    kmask_ref,
    fmask_ref,
    hout_ref,
    gout_ref,
    wout_ref,
    w2out_ref,
    vecout_ref,
    G,
    dG,
    recvC,
    R1,
    R2,
    R3,
    fin,
    xin,
    xout,
    xfin,
    vsum,
    vrecv,
    VB,
    gsum,
    grecv,
    H,
    PK,
    QK,
    PKF,
    MX,
    MXF,
    LSE,
    LSEF,
    osend,
    upsend,
    uprecv,
    dsend,
    drecv,
    kh,
    vh,
    tr,
    DK,
    DV,
    abuf,
    dnbuf,
    dacc,
    g_ref,
    a2a_s,
    a2a_r,
    ag_s,
    ag_r,
    agc_s,
    agc_r,
    rs_s,
    rs_r,
    rsc_s,
    rsc_r,
    xs_s,
    xs_r,
    v_s,
    v_r,
    gv_s,
    gv_r,
):
    dp = lax.axis_index("dp")
    fs = lax.axis_index("fsdp")
    me = {"z": lax.div(dp, 2), "c": lax.rem(dp, 2), "y": lax.div(fs, 4), "x": lax.rem(fs, 4)}

    def device(at):
        return (at["z"] * 2 + at["c"], at["y"] * 4 + at["x"])

    def beside(axis, step):
        at = dict(me)
        at[axis] = lax.rem(me[axis] + step, 2 if axis == "c" else 4)
        return at

    def remote(src, dst, send, recv, at):
        return pltpu.make_async_remote_copy(
            src_ref=src,
            dst_ref=dst,
            send_sem=send,
            recv_sem=recv,
            device_id=device(at),
            device_id_type=MESH,
        )

    barrier = pltpu.get_barrier_semaphore()

    def greet(k, carry):
        at = dict(me)
        at["y"] = lax.rem(me["y"] + lax.div(k, 4), 4)
        at["x"] = lax.rem(me["x"] + lax.rem(k, 4), 4)
        pl.semaphore_signal(barrier, inc=1, device_id=device(at), device_id_type=MESH)
        return carry

    lax.fori_loop(1, 16, greet, 0)
    for step in (1, 2, 3):
        pl.semaphore_signal(barrier, inc=1, device_id=device(beside("z", step)), device_id_type=MESH)
    pl.semaphore_signal(barrier, inc=1, device_id=device(beside("c", 1)), device_id_type=MESH)
    pl.semaphore_wait(barrier, 19)

    def x_copies():
        return [
            remote(
                blocks_ref.at[beside("x", d)["x"]],
                xin.at[me["x"]],
                xs_s.at[0, d - 1],
                xs_r.at[0, d - 1],
                beside("x", d),
            )
            for d in (1, 2, 3)
        ]

    def vec_copies(axis, buf, recv, ss, rs, slot):
        return [
            remote(buf, recv.at[slot, d - 1], ss.at[slot, d - 1], rs.at[slot, d - 1], beside(axis, d))
            for d in ((1,) if axis == "c" else (1, 2, 3))
        ]

    def held(ref, at, cols):
        return ref.at[at["z"], at["c"], at["y"], at["x"], :, pl.ds(cols[0], cols[1] - cols[0])]

    ALL = slice(None)

    def ag_copies(group, phase):
        layer, streams = AG_GROUPS[group]
        Gl = G.at[layer]
        if phase == 3:
            part = held(
                Gl, dict(z=ALL, c=me["c"], y=ALL, x=ALL), (streams[0][0], streams[2][1])
            )
            return [remote(part, part, agc_s.at[group], agc_r.at[group], beside("c", 1))]
        out = []
        for s, cols in enumerate(streams):
            order = AG_ORDERS[s]
            at = dict(me)
            for axis in order[:phase]:
                at[axis] = ALL
            part = held(Gl, at, cols)
            for d in (1, 2, 3):
                n = phase * 3 + d - 1
                out.append(
                    remote(
                        part,
                        part,
                        ag_s.at[group, s, n],
                        ag_r.at[group, s, n],
                        beside(order[phase], d),
                    )
                )
        return out

    def start(copies):
        for copy in copies:
            copy.start()

    def arrive(copies):
        for copy in copies:
            copy.wait_recv()

    def leave(copies):
        for copy in copies:
            copy.wait_send()

    def ag_step(group, phase):
        if phase > 0:
            arrive(ag_copies(group, phase - 1))
        if phase < 4:
            start(ag_copies(group, phase))

    def a2a_each(n, src, dst, act):
        def one(k, carry):
            at = dict(me)
            at["y"] = lax.rem(me["y"] + lax.div(k, 4), 4)
            at["x"] = lax.rem(me["x"] + lax.rem(k, 4), 4)
            act(remote(src(at["y"], at["x"]), dst, a2a_s.at[n, k], a2a_r.at[n, k], at))
            return carry

        lax.fori_loop(1, 16, one, 0)

    def a2a_start(n, src, dst):
        a2a_each(n, src, dst, lambda c: c.start())
        dst[...] = src(me["y"], me["x"])[...]

    def a2a_wait(n, src, dst):
        a2a_each(n, src, dst, lambda c: c.wait())

    def vector(layer, j):
        return VB[layer * VECS + j]

    def ln_parts(v):
        mean = jnp.mean(v, axis=-1, keepdims=True)
        cen = v - mean
        r = lax.rsqrt(jnp.mean(cen * cen, axis=-1, keepdims=True) + EPS)
        return cen * r, r

    def ln_forward(layer, k):
        gain = vector(layer, k)

        def rows(i, carry):
            at = pl.ds(pl.multiple_of(i * 64, 64), 64)
            hat, unused = ln_parts(H[layer, k, at, :])
            abuf[at, :] = (hat * gain).astype(BF16)
            return carry

        lax.fori_loop(0, 4, rows, 0)

    def ln_backward(layer, k):
        gain = vector(layer, k)

        def rows(i, total):
            at = pl.ds(pl.multiple_of(i * 64, 64), 64)
            hat, r = ln_parts(H[layer, k, at, :])
            dy = dacc[at, :]
            t = dy * gain
            back = r * (
                t
                - jnp.mean(t, axis=-1, keepdims=True)
                - hat * jnp.mean(t * hat, axis=-1, keepdims=True)
            )
            g_ref[at, :] = g_ref[at, :] + back
            return total + colsum(dy * hat)

        put_vector(layer, k, lax.fori_loop(0, 4, rows, jnp.zeros((1, DIM), F32)))

    def put_vector(layer, j, row):
        for t in range(4):
            at = (layer * VECS + j) * 4 + t
            gsum[at : at + 1, :] = row[:, t * 128 : (t + 1) * 128]

    def weight_cols(layer, g, first, width):
        return G[layer, :, :, :, g, :, first : first + width].reshape(DIM, width)

    def out_matrix(layer, k):
        return jnp.concatenate([weight_cols(layer, g, OUT[k], 128) for g in range(4)], axis=1)

    def project(layer, k, dst):
        def cols(g, carry):
            dst[:, g] = (
                dot(abuf[...], weight_cols(layer, g, QKV[k], 384)).astype(BF16).reshape(4, 64, 384)
            )
            return carry

        lax.fori_loop(0, 4, cols, 0)

    def join(mx):
        return jnp.concatenate([mx[:, p].reshape(TOK, 128) for p in range(4)], axis=1)

    def attention_out(layer, k, mx):
        H[layer, k + 1] = (
            H[layer, k] + dot(join(mx), out_matrix(layer, k)) + vector(layer, 3 + k)
        )

    def head_lanes(shape, h):
        where = lane(shape)
        return (where >= h * 64) & (where < (h + 1) * 64)

    def sample_prepare(layer, backward):
        k = QK[layer, :, :, 128:256].reshape(1024, 128)
        v = QK[layer, :, :, 256:384].reshape(1024, 128)
        where = lane((1024, 128))
        zero = jnp.zeros((1024, 128), BF16)
        for h in range(2):
            mine = head_lanes((1024, 128), h)
            kh[h] = jnp.where(mine, k, jnp.where(where == 64 * (1 - h), kmask_ref[...], zero))
            if backward:
                vh[h] = jnp.where(mine, v, zero)
        tr[...] = turned(k if backward else v)

    def sample_query(layer, i):
        return QK[layer, pl.ds(i * 4, 4), :, 0:128].reshape(256, 128) * jnp.asarray(SCALE, BF16)

    def with_one(q, h):
        return jnp.where(lane((256, 128)) == 64 * (1 - h), jnp.ones((256, 128), BF16), q)

    def sample_forward(layer):
        sample_prepare(layer, False)

        def block(i, carry):
            q = sample_query(layer, i)
            parts = []
            for h in range(2):
                s = dot_nt(kh[h], with_one(q, h))
                top = jnp.max(s, axis=0, keepdims=True)
                e = jnp.exp(s - top)
                total = colsum(e)
                LSE[layer, h, i] = top + jnp.log(total)
                parts.append(dot(tr[h * 64 : (h + 1) * 64, :], e.astype(BF16)) / total)
            mixed = jnp.concatenate(parts, axis=0).T.astype(BF16)
            osend[pl.ds(i * 4, 4)] = mixed.reshape(4, 64, 128)
            return carry

        lax.fori_loop(0, 4, block, 0)

    def sample_backward(layer):
        sample_prepare(layer, True)

        def block(i, carry):
            q = sample_query(layer, i)
            up = uprecv[layer, pl.ds(i * 4, 4)].reshape(256, 128)
            parts = []
            for h in range(2):
                s = dot_nt(kh[h], with_one(q, h))
                p = jnp.exp(s - LSE[layer, h, i])
                dprobs = dot_nt(vh[h], up)
                t = p * dprobs
                ds = (t - p * colsum(t)).astype(BF16)
                dv = dot(p.astype(BF16), up)
                dk = dot(ds, q)

                @pl.when(i == 0)
                def _():
                    DV[h] = dv
                    DK[h] = dk

                @pl.when(i > 0)
                def _():
                    DV[h] = DV[h] + dv
                    DK[h] = DK[h] + dk

                parts.append(dot(tr[h * 64 : (h + 1) * 64, :], ds))
            dq = (jnp.concatenate(parts, axis=0).T * SCALE).astype(BF16)
            dsend[pl.ds(i * 4, 4), :, 0:128] = dq.reshape(4, 64, 128)
            return carry

        lax.fori_loop(0, 4, block, 0)
        first = head_lanes((1024, 128), 0)
        dsend[:, :, 128:256] = jnp.where(first, DK[0], DK[1]).astype(BF16).reshape(16, 64, 128)
        dsend[:, :, 256:384] = jnp.where(first, DV[0], DV[1]).astype(BF16).reshape(16, 64, 128)

    def feature_parts(layer, p):
        q = PKF[layer, :, p, :, 0:128].reshape(TOK, 128) * jnp.asarray(SCALE, BF16)
        k = PKF[layer, :, p, :, 128:256].reshape(TOK, 128)
        v = PKF[layer, :, p, :, 256:384].reshape(TOK, 128)
        return q, k, v

    def feature_forward(layer):
        zero = jnp.zeros((TOK, 128), BF16)

        def pair(p, carry):
            q, k, v = feature_parts(layer, p)
            vt = turned(v)
            parts = []
            for h in range(2):
                mine = head_lanes((TOK, 128), h)
                s = dot_nt(jnp.where(mine, k, zero), q) + fmask_ref[...]
                top = jnp.max(s, axis=0, keepdims=True)
                e = jnp.exp(s - top)
                total = colsum(e)
                LSEF[layer, h, p] = top + jnp.log(total)
                parts.append(dot(vt[h * 64 : (h + 1) * 64, :], e.astype(BF16)) / total)
            MXF[layer, :, p] = jnp.concatenate(parts, axis=0).T.astype(BF16).reshape(4, 64, 128)
            return carry

        lax.fori_loop(0, 4, pair, 0)

    def feature_backward(layer):
        zero = jnp.zeros((TOK, 128), BF16)

        def pair(p, carry):
            q, k, v = feature_parts(layer, p)
            up = upsend[:, p].reshape(TOK, 128)
            kt = turned(k)
            dqs, dks, dvs = [], [], []
            for h in range(2):
                mine = head_lanes((TOK, 128), h)
                s = dot_nt(jnp.where(mine, k, zero), q) + fmask_ref[...]
                probs = jnp.exp(s - LSEF[layer, h, p])
                dprobs = dot_nt(jnp.where(mine, v, zero), up)
                t = probs * dprobs
                ds = (t - probs * colsum(t)).astype(BF16)
                dvs.append(dot(probs.astype(BF16), up))
                dks.append(dot(ds, q))
                dqs.append(dot(kt[h * 64 : (h + 1) * 64, :], ds))
            first = head_lanes((TOK, 128), 0)
            dq = (jnp.concatenate(dqs, axis=0).T * SCALE).astype(BF16)
            drecv[:, p, :, 0:128] = dq.reshape(4, 64, 128)
            dk = jnp.where(first, dks[0], dks[1]).astype(BF16)
            drecv[:, p, :, 128:256] = dk.reshape(4, 64, 128)
            dv = jnp.where(first, dvs[0], dvs[1]).astype(BF16)
            drecv[:, p, :, 256:384] = dv.reshape(4, 64, 128)
            return carry

        lax.fori_loop(0, 4, pair, 0)

    def outer_block(layer, g):
        return G[layer, g, :, :, :, :, OUTER : OUTER + 512].reshape(DIM, DIM)

    def gelu_parts(pre):
        inner = 0.7978845608028654 * (pre + 0.044715 * (pre * pre * pre))
        th = jnp.tanh(inner)
        return th

    def ff_forward(layer, last):
        ln_forward(layer, 2)
        dacc[...] = H[layer, 2] + vector(layer, 5)

        def cols(g, carry):
            pre = dot(abuf[...], weight_cols(layer, g, INNER, 512)) + VB[layer * VECS + 6 + g]
            act = (0.5 * pre * (1.0 + gelu_parts(pre))).astype(BF16)
            dacc[...] = dacc[...] + dot(act, outer_block(layer, g))
            return carry

        lax.fori_loop(0, 4, cols, 0)
        if last:
            hout_ref[...] = dacc[...]
        else:
            H[layer + 1, 0] = dacc[...]

    def round_gradient(layer, j):
        down = g_ref[...].astype(BF16)
        dnbuf[...] = down
        put_vector(layer, j, colsum(down.astype(F32)))

    def ff_backward(layer):
        round_gradient(layer, 5)
        ln_forward(layer, 2)

        def cols(g, carry):
            w1 = weight_cols(layer, g, INNER, 512)
            pre = dot(abuf[...], w1) + VB[layer * VECS + 6 + g]
            th = gelu_parts(pre)
            half = 0.5 * (1.0 + th)
            act = (pre * half).astype(BF16)
            slope = half + 0.5 * pre * (1.0 - th * th) * (
                0.7978845608028654 * (1.0 + 3 * 0.044715 * (pre * pre))
            )
            dact = dot_nt(dnbuf[...], outer_block(layer, g))
            dpre = (dact * slope).astype(BF16)
            dG[layer, g, :, :, :, :, OUTER : OUTER + 512] = (
                dot(turned(act), dnbuf[...]).astype(BF16).reshape(2, 4, 4, 16, 512)
            )
            dG[layer, :, :, :, g, :, INNER : INNER + 512] = (
                dot(turned(abuf[...]), dpre).astype(BF16).reshape(4, 2, 4, 16, 512)
            )
            dc = dot_nt(dpre, w1)

            @pl.when(g == 0)
            def _():
                dacc[...] = dc

            @pl.when(g > 0)
            def _():
                dacc[...] = dacc[...] + dc

            row = colsum(dpre.astype(F32))
            for t in range(4):
                gsum[pl.ds((layer * VECS + 6 + g) * 4 + t, 1), :] = row[:, t * 128 : (t + 1) * 128]
            return carry

        lax.fori_loop(0, 4, cols, 0)
        ln_backward(layer, 2)

    def attention_out_backward(layer, k, mx):
        round_gradient(layer, 3 + k)
        down = dnbuf[...]
        dwo = dot(turned(join(mx)), down).astype(BF16)
        for g in range(4):
            dG[layer, :, :, :, g, :, OUT[k] : OUT[k] + 128] = dwo[:, g * 128 : (g + 1) * 128].reshape(
                4, 2, 4, 16, 128
            )
        up = dot_nt(down, out_matrix(layer, k)).astype(BF16)
        for p in range(4):
            upsend[:, p] = up[:, p * 128 : (p + 1) * 128].reshape(4, 64, 128)

    def project_backward(layer, k):
        ln_forward(layer, k)
        at = turned(abuf[...])

        def cols(g, carry):
            d = drecv[:, g].reshape(TOK, 384)
            w = weight_cols(layer, g, QKV[k], 384)
            dG[layer, :, :, :, g, :, QKV[k] : QKV[k] + 384] = (
                dot(at, d).astype(BF16).reshape(4, 2, 4, 16, 384)
            )
            da = dot_nt(d, w)

            @pl.when(g == 0)
            def _():
                dacc[...] = da

            @pl.when(g > 0)
            def _():
                dacc[...] = dacc[...] + da

            return carry

        lax.fori_loop(0, 4, cols, 0)
        ln_backward(layer, k)

    def rest(order, phase):
        return "".join(a for a in "zyx" if a not in order[:phase])

    def rs_copies(layer, group, phase):
        streams = RS_GROUPS[group]
        n = layer * 3 + group
        if phase == 0:
            cols = (streams[0][0], streams[2][1])
            src = held(dG.at[layer], dict(z=ALL, c=beside("c", 1)["c"], y=ALL, x=ALL), cols)
            dst = recvC.at[:, :, :, :, pl.ds(cols[0], cols[1] - cols[0])]
            return [remote(src, dst, rsc_s.at[n], rsc_r.at[n], beside("c", 1))]
        out = []
        for s, cols in enumerate(streams):
            order = RS_ORDERS[s]
            window = pl.ds(cols[0], cols[1] - cols[0])
            for d in (1, 2, 3):
                peer = beside(order[phase - 1], d)
                at = dict(z=ALL, c=me["c"], y=ALL, x=ALL)
                for axis in order[: phase - 1]:
                    at[axis] = me[axis]
                at[order[phase - 1]] = peer[order[phase - 1]]
                src = held(dG.at[layer], at, cols)
                if phase == 1:
                    dst = R1.at[d - 1, :, :, :, window]
                elif phase == 2:
                    dst = R2.at[layer, d - 1, :, :, window]
                else:
                    dst = R3.at[layer, d - 1, :, window]
                m = (phase - 1) * 3 + d - 1
                out.append(remote(src, dst, rs_s.at[n, s, m], rs_r.at[n, s, m], peer))
        return out

    def rs_sum(layer, group, phase):
        streams = RS_GROUPS[group]
        if phase == 0:
            first, last = streams[0][0], streams[2][1]

            def add(i, carry):
                z, y = lax.div(i, 4), lax.rem(i, 4)
                mine = dG[layer, z, me["c"], y, :, :, first:last].astype(F32)
                other = recvC[z, y, :, :, first:last].astype(F32)
                dG[layer, z, me["c"], y, :, :, first:last] = (mine + other).astype(BF16)
                return carry

            lax.fori_loop(0, 16, add, 0)
            return
        for s, (first, last) in enumerate(streams):
            order = RS_ORDERS[s]
            left = rest(order, phase)
            if phase == 1:

                def add(i, carry, left=left, order=order, first=first, last=last):
                    u = lax.div(i, 4)
                    v = lax.rem(i, 4)
                    at = {left[0]: u, left[1]: v, order[0]: me[order[0]]}
                    total = dG[layer, at["z"], me["c"], at["y"], at["x"], :, first:last].astype(F32)
                    for d in range(3):
                        total = total + R1[d, u, v, :, first:last].astype(F32)
                    dG[layer, at["z"], me["c"], at["y"], at["x"], :, first:last] = total.astype(BF16)
                    return carry

                lax.fori_loop(0, 16, add, 0)
            elif phase == 2:

                def add(u, carry, left=left, order=order, first=first, last=last):
                    at = dict(me)
                    at[left[0]] = u
                    total = dG[layer, at["z"], me["c"], at["y"], at["x"], :, first:last].astype(F32)
                    for d in range(3):
                        total = total + R2[layer, d, u, :, first:last].astype(F32)
                    dG[layer, at["z"], me["c"], at["y"], at["x"], :, first:last] = total.astype(BF16)
                    return carry

                lax.fori_loop(0, 4, add, 0)
            else:
                total = dG[layer, me["z"], me["c"], me["y"], me["x"], :, first:last].astype(F32)
                for d in range(3):
                    total = total + R3[layer, d, :, first:last].astype(F32)
                fin[layer, :, first:last] = total

    def rs_step(layer, group, phase):
        if phase > 0:
            copies = rs_copies(layer, group, phase - 1)
            arrive(copies)
            leave(copies)
            rs_sum(layer, group, phase - 1)
        if phase < 4:
            start(rs_copies(layer, group, phase))

    start(x_copies())
    vsum[...] = vec_ref[...]
    start(vec_copies("x", vsum, vrecv, v_s, v_r, 0))
    xin[me["x"]] = blocks_ref[me["x"]]
    for layer in range(LAYERS):
        G[layer, me["z"], me["c"], me["y"], me["x"], :, OUTER : OUTER + 512] = outer_ref[layer]
    H[0, 0] = x_ref[...].astype(F32)
    row = lax.broadcasted_iota(jnp.int32, (64, 64), 0)
    col = lax.broadcasted_iota(jnp.int32, (64, 64), 1)

    def swap_groups(v):
        return (v & 3) | ((v & 12) << 2) | ((v & 48) >> 2)

    perm = jnp.where(swap_groups(row) == col, 1.0, 0.0).astype(BF16)
    arrive(x_copies())
    mixed_rows = dot(perm, xin[...].reshape(64, 768)).astype(BF16)
    for layer in range(LAYERS):
        for kk in range(4):
            G[layer, me["z"], me["c"], me["y"], me["x"], :, kk * 384 : (kk + 1) * 384] = mixed_rows[
                kk * 16 : (kk + 1) * 16, layer * 384 : (layer + 1) * 384
            ]
    ag_step(0, 0)

    def vec_sum(buf, recv, copies, slot, count):
        arrive(copies)
        leave(copies)
        total = buf[...].astype(F32)
        for d in range(count):
            total = total + recv[slot, d].astype(F32)
        buf[...] = total.astype(buf.dtype)

    vec_sum(vsum, vrecv, vec_copies("x", vsum, vrecv, v_s, v_r, 0), 0, 3)
    start(vec_copies("y", vsum, vrecv, v_s, v_r, 1))
    ag_step(0, 1)
    ag_step(1, 0)
    vec_sum(vsum, vrecv, vec_copies("y", vsum, vrecv, v_s, v_r, 1), 1, 3)
    start(vec_copies("z", vsum, vrecv, v_s, v_r, 2))
    ag_step(0, 2)
    ag_step(1, 1)
    vec_sum(vsum, vrecv, vec_copies("z", vsum, vrecv, v_s, v_r, 2), 2, 3)
    start(vec_copies("c", vsum, vrecv, v_s, v_r, 3))
    vec_sum(vsum, vrecv, vec_copies("c", vsum, vrecv, v_s, v_r, 3), 3, 1)
    vecs = vsum[...].astype(F32)
    for j in range(LAYERS * VECS):
        VB[j] = jnp.concatenate([vecs[4 * j + t : 4 * j + t + 1, :] for t in range(4)], axis=1)
    ag_step(0, 3)
    ln_forward(0, 0)
    ag_step(0, 4)

    def fsrc(y, x):
        return PK.at[y, x]

    def osrc(y, x):
        return osend.at[y * 4 + x]

    def usrc(y, x):
        return upsend.at[y, x]

    def dsrc(y, x):
        return dsend.at[y * 4 + x]

    for layer in range(LAYERS):
        if layer > 0:
            ln_forward(layer, 0)
        project(layer, 0, PK)
        a2a_start(layer * 4, fsrc, QK.at[layer, fs])
        if layer == 0:
            ag_step(1, 2)
        a2a_wait(layer * 4, fsrc, QK.at[layer, fs])
        sample_forward(layer)
        a2a_start(layer * 4 + 1, osrc, MX.at[layer, me["y"], me["x"]])
        if layer == 0:
            ag_step(1, 3)
            ag_step(2, 0)
        a2a_wait(layer * 4 + 1, osrc, MX.at[layer, me["y"], me["x"]])
        if layer == 0:
            ag_step(1, 4)
            ag_step(2, 1)
        attention_out(layer, 0, MX.at[layer])
        ln_forward(layer, 1)
        project(layer, 1, PKF.at[layer])
        if layer == 0:
            ag_step(2, 2)
        feature_forward(layer)
        attention_out(layer, 1, MXF.at[layer])
        ff_forward(layer, layer == LAYERS - 1)
        if layer == 0:
            ag_step(2, 3)
            ag_step(2, 4)

    g_ref[...] = seed_ref[...].astype(F32)
    for layer in (1, 0):
        ff_backward(layer)
        if layer == 0:
            rs_step(1, 2, 1)
        rs_step(layer, 0, 0)
        if layer == 0:
            rs_step(1, 1, 3)
        attention_out_backward(layer, 1, MXF.at[layer])
        feature_backward(layer)
        rs_step(layer, 0, 1)
        if layer == 0:
            rs_step(1, 2, 2)
            rs_step(1, 1, 4)
        project_backward(layer, 1)
        rs_step(layer, 1, 0)
        attention_out_backward(layer, 0, MX.at[layer])
        a2a_start(layer * 4 + 2, usrc, uprecv.at[layer, fs])
        rs_step(layer, 0, 2)
        if layer == 0:
            rs_step(1, 2, 3)
        a2a_wait(layer * 4 + 2, usrc, uprecv.at[layer, fs])
        sample_backward(layer)
        a2a_start(layer * 4 + 3, dsrc, drecv.at[me["y"], me["x"]])
        rs_step(layer, 0, 3)
        rs_step(layer, 1, 1)
        if layer == 0:
            rs_step(1, 2, 4)
        a2a_wait(layer * 4 + 3, dsrc, drecv.at[me["y"], me["x"]])
        project_backward(layer, 0)
        rs_step(layer, 2, 0)
        rs_step(layer, 1, 2)
        rs_step(layer, 0, 4)
    gout_ref[...] = g_ref[...]

    gv = functools.partial(vec_copies, buf=gsum, recv=grecv, ss=gv_s, rs=gv_r)
    start(gv("x", slot=0))
    rs_step(0, 2, 1)
    vec_sum(gsum, grecv, gv("x", slot=0), 0, 3)
    start(gv("y", slot=1))
    rs_step(0, 1, 3)
    rs_step(0, 2, 2)
    vec_sum(gsum, grecv, gv("y", slot=1), 1, 3)
    start(gv("z", slot=2))
    rs_step(0, 1, 4)
    rs_step(0, 2, 3)
    vec_sum(gsum, grecv, gv("z", slot=2), 2, 3)
    start(gv("c", slot=3))
    rs_step(0, 2, 4)
    vec_sum(gsum, grecv, gv("c", slot=3), 3, 1)
    vecout_ref[...] = gsum[...]
    w2out_ref[...] = fin[:, :, OUTER : OUTER + 512]
    stacked = jnp.concatenate(
        [
            jnp.concatenate([fin[l, :, kk * 384 : (kk + 1) * 384] for l in range(LAYERS)], axis=1)
            for kk in range(4)
        ],
        axis=0,
    ).astype(BF16)
    xout[...] = dot(perm, stacked).astype(BF16).reshape(4, 16, 768)

    def xf_copies():
        return [
            remote(
                xout.at[beside("x", d)["x"]],
                xfin.at[me["x"]],
                xs_s.at[1, d - 1],
                xs_r.at[1, d - 1],
                beside("x", d),
            )
            for d in (1, 2, 3)
        ]

    start(xf_copies())
    xfin[me["x"]] = xout[me["x"]]
    arrive(xf_copies())
    wout_ref[...] = xfin[...].astype(F32)
    leave(xf_copies())
    leave(x_copies())
    for group in range(3):
        for phase in range(4):
            leave(ag_copies(group, phase))


def vmem(shape, dtype):
    return pltpu.VMEM(shape, dtype)


def layers(x, seed, blocks, outer, vec, kmask, fmask):
    dma = pltpu.SemaphoreType.DMA
    whole = pl.BlockSpec(memory_space=pltpu.VMEM)
    return pl.pallas_call(
        kernel,
        out_shape=(
            jax.ShapeDtypeStruct((TOK, DIM), F32),
            jax.ShapeDtypeStruct((TOK, DIM), F32),
            jax.ShapeDtypeStruct((4, 16, 768), F32),
            jax.ShapeDtypeStruct((LAYERS, 16, 512), F32),
            jax.ShapeDtypeStruct((80, 128), F32),
        ),
        in_specs=[whole] * 7,
        out_specs=(whole,) * 5,
        scratch_shapes=[
            vmem((2, 4, 2, 4, 4, 16, 2048), BF16),
            vmem((2, 4, 2, 4, 4, 16, 2048), BF16),
            vmem((4, 4, 4, 16, 2048), BF16),
            vmem((3, 4, 4, 16, 2048), BF16),
            vmem((2, 3, 4, 16, 2048), BF16),
            vmem((2, 3, 16, 2048), BF16),
            vmem((2, 16, 2048), F32),
            vmem((4, 16, 768), BF16),
            vmem((4, 16, 768), BF16),
            vmem((4, 16, 768), BF16),
            vmem((80, 128), BF16),
            vmem((4, 3, 80, 128), BF16),
            vmem((20, 1, 512), F32),
            vmem((80, 128), F32),
            vmem((4, 3, 80, 128), F32),
            vmem((2, 3, TOK, DIM), F32),
            vmem((4, 4, 64, 384), BF16),
            vmem((2, 16, 64, 384), BF16),
            vmem((2, 4, 4, 64, 384), BF16),
            vmem((2, 4, 4, 64, 128), BF16),
            vmem((2, 4, 4, 64, 128), BF16),
            vmem((2, 2, 4, 1, 256), F32),
            vmem((2, 2, 4, 1, 256), F32),
            vmem((16, 64, 128), BF16),
            vmem((4, 4, 64, 128), BF16),
            vmem((2, 16, 64, 128), BF16),
            vmem((16, 64, 384), BF16),
            vmem((4, 4, 64, 384), BF16),
            vmem((2, 1024, 128), BF16),
            vmem((2, 1024, 128), BF16),
            vmem((128, 1024), BF16),
            vmem((2, 1024, 128), F32),
            vmem((2, 1024, 128), F32),
            vmem((TOK, DIM), BF16),
            vmem((TOK, DIM), BF16),
            vmem((TOK, DIM), F32),
            vmem((TOK, DIM), F32),
            dma((8, 16)),
            dma((8, 16)),
            dma((3, 3, 9)),
            dma((3, 3, 9)),
            dma((3,)),
            dma((3,)),
            dma((6, 3, 9)),
            dma((6, 3, 9)),
            dma((6,)),
            dma((6,)),
            dma((2, 3)),
            dma((2, 3)),
            dma((4, 3)),
            dma((4, 3)),
            dma((4, 3)),
            dma((4, 3)),
        ],
        compiler_params=pltpu.CompilerParams(
            collective_id=0, has_side_effects=True, vmem_limit_bytes=63 * 2**20
        ),
    )(x, seed, blocks, outer, vec, kmask, fmask)


def body(
    entry_embeddings,
    norm_scales,
    triple_entry_matrix,
    mixing_exit_matrix,
    exit_bias,
    expanding_matrix,
    former_dense_bias,
    contracting_matrix,
    latter_dense_bias,
    row_presence_indicator,
    problem_column_number,
    loss_gradient,
):
    fs = lax.axis_index("fsdp")
    me = lax.axis_index("dp") * 16 + fs
    sample_ok = row_presence_indicator[0] > 0
    local_ok = lax.dynamic_slice_in_dim(sample_ok, fs * 64, 64)
    feature_ok = jnp.arange(4, dtype=jnp.int32) < problem_column_number[0]
    keep = feature_ok[:, None] & local_ok[None, :]

    x = entry_embeddings[0].transpose(1, 0, 2).reshape(TOK, DIM)
    seed = loss_gradient[0].transpose(1, 0, 2)
    seed = jnp.where(keep[:, :, None], seed, jnp.zeros_like(seed)).reshape(TOK, DIM)

    heads = triple_entry_matrix.reshape(2, 2, 4, 3, 4, 128)
    merge = mixing_exit_matrix.reshape(2, 2, 4, 1, 4, 128)
    chunks = jnp.concatenate([heads, merge], axis=3)
    chunks = chunks.transpose(4, 0, 2, 1, 3, 5).reshape(4, 2, 4, 8, 128)
    inner = expanding_matrix.reshape(2, 4, 4, 4, 128).transpose(2, 0, 1, 3, 4)
    chunks = jnp.concatenate([chunks, inner], axis=3).reshape(4, 2, 4, 4, 3, 128)
    blocks = chunks.transpose(0, 3, 2, 1, 4, 5).reshape(4, 16, 768)

    small = jnp.concatenate([norm_scales, exit_bias, latter_dense_bias[:, None]], axis=1)
    place = jnp.arange(512, dtype=jnp.int32) // 4 == me
    small = jnp.where(place, jnp.tile(small, (1, 1, 128)), 0).reshape(2, 24, 128)
    place = jnp.arange(2048, dtype=jnp.int32) // 16 == me
    large = jnp.where(place, jnp.tile(former_dense_bias, (1, 128)), 0).reshape(2, 16, 128)
    vec = jnp.concatenate([small, large], axis=1).reshape(80, 128).astype(BF16)

    kmask = jnp.where(sample_ok[:, None], 0.0, NEG).astype(BF16)
    kmask = jnp.broadcast_to(kmask, (1024, 128))
    key = jnp.arange(TOK, dtype=jnp.int32)
    same = (key[:, None] % 64 == key[None, :] % 64) & (key // 64 < problem_column_number[0])[:, None]
    fmask = jnp.where(same, 0.0, NEG).astype(F32)

    h, g, w, w2, vecs = layers(x, seed, blocks, contracting_matrix, vec, kmask, fmask)

    h = jnp.where(keep[:, :, None], h.reshape(4, 64, DIM), 0.0).transpose(1, 0, 2)
    g = g.reshape(4, 64, DIM).transpose(1, 0, 2)
    w = w.reshape(4, 4, 4, 2, 3, 128)
    w = w.transpose(3, 2, 1, 4, 0, 5).reshape(2, 4, 12, 4, 128)
    delta_heads = jnp.stack(
        [w[:, :, 0:3].reshape(2, 4, 1536), w[:, :, 4:7].reshape(2, 4, 1536)], axis=1
    )
    delta_merge = jnp.stack([w[:, :, 3].reshape(2, 4, 512), w[:, :, 7].reshape(2, 4, 512)], axis=1)
    delta_inner = w[:, :, 8:12].transpose(0, 1, 3, 2, 4).reshape(2, 4, 2048)
    vecs = vecs.reshape(2, 40 * 128)
    small = lax.dynamic_slice_in_dim(vecs[:, : 6 * 512].reshape(2, 6, 512), me * 4, 4, 2)
    thresholds = lax.dynamic_slice_in_dim(vecs[:, 6 * 512 :], me * 16, 16, 1)
    return (
        h[None],
        g[None],
        small[:, 0:3],
        delta_heads,
        delta_merge,
        small[:, 3:5],
        delta_inner,
        thresholds,
        w2,
        small[:, 5],
    )


def solution(mesh):
    both = ("dp", "fsdp")
    tokens = P("dp", "fsdp", None, None)
    weights = (
        P(None, None, both),
        P(None, None, both, None),
        P(None, None, both, None),
        P(None, None, both),
        P(None, both, None),
        P(None, both),
        P(None, both, None),
        P(None, both),
    )
    return jax.shard_map(
        body,
        mesh=mesh,
        in_specs=(tokens,) + weights + (P("dp", None), P("dp"), tokens),
        out_specs=(tokens, tokens) + weights,
        check_vma=False,
    )
```

```python
import functools

import jax
import jax.numpy as jnp
from jax import lax
from jax.experimental import pallas as pl
from jax.experimental.pallas import tpu as pltpu
from jax.sharding import PartitionSpec as P

EPS = 1e-05
NEG = -1e30
F32 = jnp.float32
BF16 = jnp.bfloat16
MESH = pl.DeviceIdType.MESH
LAYERS = 2
TOK = 256
DIM = 512
VECS = 10
SCALE = 0.125

QKV = (0, 512)
OUT = (384, 896)
INNER = 1024
OUTER = 1536

AG_ORDERS = ("xyz", "yzx", "zxy")
AG_GROUPS = (
    (0, ((0, 128), (128, 256), (256, 384))),
    (0, ((384, 1024), (1024, 1536), (1536, 2048))),
    (1, ((0, 128), (128, 256), (256, 384))),
    (1, ((384, 1024), (1024, 1536), (1536, 2048))),
)
RS_ORDERS = ("zyx", "xzy", "yxz")
RS_GROUPS = (
    ((1024, 1280), (1280, 1664), (1664, 2048)),
    ((384, 640), (640, 896), (896, 1024)),
    ((0, 128), (128, 256), (256, 384)),
)


def dot(a, b):
    return jnp.dot(a, b, preferred_element_type=F32)


def dot_nt(a, b):
    return lax.dot_general(a, b, (((1,), (1,)), ((), ())), preferred_element_type=F32)


def turned(a):
    return a.astype(F32).T.astype(BF16)


def colsum(a):
    return jnp.sum(a, axis=0, keepdims=True)


def lane(shape):
    return lax.broadcasted_iota(jnp.int32, shape, len(shape) - 1)


def kernel(
    x_ref,
    seed_ref,
    blocks_ref,
    outer_ref,
    vec_ref,
    kmask_ref,
    fmask_ref,
    hout_ref,
    gout_ref,
    wout_ref,
    w2out_ref,
    vecout_ref,
    G,
    dG,
    recvC,
    R1,
    R2,
    R3,
    fin,
    xin,
    xout,
    xfin,
    vsum,
    vrecv,
    VB,
    gsum,
    grecv,
    H,
    PK,
    QK,
    PKF,
    MX,
    MXF,
    LSE,
    LSEF,
    osend,
    upsend,
    uprecv,
    dqsend,
    dsend,
    drecv,
    dfeat,
    kh,
    vh,
    tr,
    DK,
    DV,
    A,
    DN,
    ACT,
    DPRE,
    dacc,
    g_ref,
    a2a_s,
    a2a_r,
    ag_s,
    ag_r,
    agc_s,
    agc_r,
    rs_s,
    rs_r,
    rsc_s,
    rsc_r,
    xs_s,
    xs_r,
    v_s,
    v_r,
    gv_s,
    gv_r,
):
    dp = lax.axis_index("dp")
    fs = lax.axis_index("fsdp")
    me = {"z": lax.div(dp, 2), "c": lax.rem(dp, 2), "y": lax.div(fs, 4), "x": lax.rem(fs, 4)}

    def device(at):
        return (at["z"] * 2 + at["c"], at["y"] * 4 + at["x"])

    def beside(axis, step):
        at = dict(me)
        at[axis] = lax.rem(me[axis] + step, 2 if axis == "c" else 4)
        return at

    def remote(src, dst, send, recv, at):
        return pltpu.make_async_remote_copy(
            src_ref=src,
            dst_ref=dst,
            send_sem=send,
            recv_sem=recv,
            device_id=device(at),
            device_id_type=MESH,
        )

    barrier = pltpu.get_barrier_semaphore()

    def greet(k, carry):
        at = dict(me)
        at["y"] = lax.rem(me["y"] + lax.div(k, 4), 4)
        at["x"] = lax.rem(me["x"] + lax.rem(k, 4), 4)
        pl.semaphore_signal(barrier, inc=1, device_id=device(at), device_id_type=MESH)
        return carry

    lax.fori_loop(1, 16, greet, 0)
    for step in (1, 2, 3):
        pl.semaphore_signal(barrier, inc=1, device_id=device(beside("z", step)), device_id_type=MESH)
    pl.semaphore_signal(barrier, inc=1, device_id=device(beside("c", 1)), device_id_type=MESH)
    pl.semaphore_wait(barrier, 19)

    def x_copies():
        return [
            remote(
                blocks_ref.at[beside("x", d)["x"]],
                xin.at[me["x"]],
                xs_s.at[0, d - 1],
                xs_r.at[0, d - 1],
                beside("x", d),
            )
            for d in (1, 2, 3)
        ]

    def vec_copies(axis, buf, recv, ss, rs, slot):
        return [
            remote(buf, recv.at[slot, d - 1], ss.at[slot, d - 1], rs.at[slot, d - 1], beside(axis, d))
            for d in ((1,) if axis == "c" else (1, 2, 3))
        ]

    def held(ref, at, cols):
        return ref.at[at["z"], at["c"], at["y"], at["x"], :, pl.ds(cols[0], cols[1] - cols[0])]

    ALL = slice(None)

    def ag_copies(group, phase):
        layer, streams = AG_GROUPS[group]
        Gl = G.at[layer]
        if phase == 3:
            part = held(
                Gl, dict(z=ALL, c=me["c"], y=ALL, x=ALL), (streams[0][0], streams[2][1])
            )
            return [remote(part, part, agc_s.at[group], agc_r.at[group], beside("c", 1))]
        out = []
        for s, cols in enumerate(streams):
            order = AG_ORDERS[s]
            at = dict(me)
            for axis in order[:phase]:
                at[axis] = ALL
            part = held(Gl, at, cols)
            for d in (1, 2, 3):
                n = phase * 3 + d - 1
                out.append(
                    remote(
                        part,
                        part,
                        ag_s.at[group, s, n],
                        ag_r.at[group, s, n],
                        beside(order[phase], d),
                    )
                )
        return out

    def start(copies):
        for copy in copies:
            copy.start()

    def arrive(copies):
        for copy in copies:
            copy.wait_recv()

    def leave(copies):
        for copy in copies:
            copy.wait_send()

    def ag_step(group, phase):
        if phase > 0:
            arrive(ag_copies(group, phase - 1))
        if phase < 4:
            start(ag_copies(group, phase))

    def plane(k):
        at = dict(me)
        at["y"] = lax.rem(me["y"] + lax.div(k, 4), 4)
        at["x"] = lax.rem(me["x"] + lax.rem(k, 4), 4)
        return at

    def a2a_one(n, k, src, dst):
        at = plane(k)
        return remote(src(at["y"], at["x"]), dst, a2a_s.at[n, k], a2a_r.at[n, k], at)

    def a2a_start(n, src, dst):
        def one(k, carry):
            a2a_one(n, k, src, dst).start()
            return carry

        lax.fori_loop(1, 16, one, 0)
        dst[...] = src(me["y"], me["x"])[...]

    def a2a_wait(n, src, dst):
        def one(k, carry):
            a2a_one(n, k, src, dst).wait()
            return carry

        lax.fori_loop(1, 16, one, 0)

    def a2a_share(n, src, dst, dy, dx):
        k = dy * 4 + dx

        @pl.when(k > 0)
        def _():
            a2a_one(n, k, src, dst).start()

        @pl.when(k == 0)
        def _():
            dst[...] = src(me["y"], me["x"])[...]

    def DG(layer):
        return dG if layer == 1 else G.at[1]

    def vector(layer, j):
        return VB[layer * VECS + j]

    def ln_parts(v):
        mean = jnp.mean(v, axis=-1, keepdims=True)
        cen = v - mean
        r = lax.rsqrt(jnp.mean(cen * cen, axis=-1, keepdims=True) + EPS)
        return cen * r, r

    def ln_forward(layer, k):
        gain = vector(layer, k)

        def rows(i, carry):
            at = pl.ds(pl.multiple_of(i * 64, 64), 64)
            hat, unused = ln_parts(H[layer, k, at, :])
            A[layer, k, at, :] = (hat * gain).astype(BF16)
            return carry

        lax.fori_loop(0, 4, rows, 0, unroll=True)

    def ln_backward(layer, k):
        gain = vector(layer, k)

        def rows(i, total):
            at = pl.ds(pl.multiple_of(i * 64, 64), 64)
            hat, r = ln_parts(H[layer, k, at, :])
            dy = dacc[at, :]
            t = dy * gain
            back = r * (
                t
                - jnp.mean(t, axis=-1, keepdims=True)
                - hat * jnp.mean(t * hat, axis=-1, keepdims=True)
            )
            g_ref[at, :] = g_ref[at, :] + back
            return total + colsum(dy * hat)

        put_vector(layer, k, lax.fori_loop(0, 4, rows, jnp.zeros((1, DIM), F32), unroll=True))

    def put_vector(layer, j, row):
        for t in range(4):
            at = (layer * VECS + j) * 4 + t
            gsum[at : at + 1, :] = row[:, t * 128 : (t + 1) * 128]

    def weight_cols(layer, g, first, width):
        return G[layer, :, :, :, g, :, first : first + width].reshape(DIM, width)

    def out_matrix(layer, k):
        return jnp.concatenate([weight_cols(layer, g, OUT[k], 128) for g in range(4)], axis=1)

    def project(layer, k, dst, then=None):
        def cols(step, carry):
            g = lax.rem(me["x"] + step, 4)
            out = dot(A[layer, k], weight_cols(layer, g, QKV[k], 384))
            dst[:, g] = out.astype(BF16).reshape(4, 64, 384)
            if then is not None:
                then(step)
            return carry

        lax.fori_loop(0, 4, cols, 0, unroll=True)

    def join(mx):
        return jnp.concatenate([mx[:, p].reshape(TOK, 128) for p in range(4)], axis=1)

    def attention_out(layer, k, mx):
        H[layer, k + 1] = (
            H[layer, k] + dot(join(mx), out_matrix(layer, k)) + vector(layer, 3 + k)
        )

    def head_lanes(shape, h):
        where = lane(shape)
        return (where >= h * 64) & (where < (h + 1) * 64)

    def sample_prepare(layer, backward):
        k = QK[layer, :, :, 128:256].reshape(1024, 128)
        v = QK[layer, :, :, 256:384].reshape(1024, 128)
        where = lane((1024, 128))
        zero = jnp.zeros((1024, 128), BF16)
        for h in range(2):
            mine = head_lanes((1024, 128), h)
            kh[h] = jnp.where(mine, k, jnp.where(where == 64 * (1 - h), kmask_ref[...], zero))
            if backward:
                vh[h] = jnp.where(mine, v, zero)
        tr[...] = turned(k if backward else v)

    def sample_query(layer, i):
        return QK[layer, pl.ds(i * 4, 4), :, 0:128].reshape(256, 128) * jnp.asarray(SCALE, BF16)

    def with_one(q, h):
        return jnp.where(lane((256, 128)) == 64 * (1 - h), jnp.ones((256, 128), BF16), q)

    def sample_forward(layer, then):
        sample_prepare(layer, False)

        def block(step, carry):
            i = lax.rem(me["y"] + step, 4)
            q = sample_query(layer, i)
            parts = []
            for h in range(2):
                s = dot_nt(kh[h], with_one(q, h))
                top = jnp.max(s, axis=0, keepdims=True)
                e = jnp.exp(s - top)
                total = colsum(e)
                LSE[layer, h, i] = top + jnp.log(total)
                parts.append(dot(tr[h * 64 : (h + 1) * 64, :], e.astype(BF16)) / total)
            mixed = jnp.concatenate(parts, axis=0).T.astype(BF16)
            osend[pl.ds(i * 4, 4)] = mixed.reshape(4, 64, 128)
            then(step)
            return carry

        lax.fori_loop(0, 4, block, 0, unroll=True)

    def sample_backward(layer, then):
        sample_prepare(layer, True)

        def block(step, carry):
            i = lax.rem(me["y"] + step, 4)
            q = sample_query(layer, i)
            up = uprecv[layer, pl.ds(i * 4, 4)].reshape(256, 128)
            parts = []
            for h in range(2):
                s = dot_nt(kh[h], with_one(q, h))
                p = jnp.exp(s - LSE[layer, h, i])
                dprobs = dot_nt(vh[h], up)
                t = p * dprobs
                ds = (t - p * colsum(t)).astype(BF16)
                dv = dot(p.astype(BF16), up)
                dk = dot(ds, q)

                @pl.when(step == 0)
                def _():
                    DV[h] = dv
                    DK[h] = dk

                @pl.when(step > 0)
                def _():
                    DV[h] = DV[h] + dv
                    DK[h] = DK[h] + dk

                parts.append(dot(tr[h * 64 : (h + 1) * 64, :], ds))
            dq = (jnp.concatenate(parts, axis=0).T * SCALE).astype(BF16)
            dqsend[pl.ds(i * 4, 4)] = dq.reshape(4, 64, 128)
            then(step)
            return carry

        lax.fori_loop(0, 4, block, 0, unroll=True)
        first = head_lanes((1024, 128), 0)
        dsend[:, :, 0:128] = jnp.where(first, DK[0], DK[1]).astype(BF16).reshape(16, 64, 128)
        dsend[:, :, 128:256] = jnp.where(first, DV[0], DV[1]).astype(BF16).reshape(16, 64, 128)

    def feature_parts(layer, p):
        q = PKF[layer, :, p, :, 0:128].reshape(TOK, 128) * jnp.asarray(SCALE, BF16)
        k = PKF[layer, :, p, :, 128:256].reshape(TOK, 128)
        v = PKF[layer, :, p, :, 256:384].reshape(TOK, 128)
        return q, k, v

    def feature_forward(layer):
        zero = jnp.zeros((TOK, 128), BF16)

        def pair(p, carry):
            q, k, v = feature_parts(layer, p)
            vt = turned(v)
            parts = []
            for h in range(2):
                mine = head_lanes((TOK, 128), h)
                s = dot_nt(jnp.where(mine, k, zero), q) + fmask_ref[...]
                top = jnp.max(s, axis=0, keepdims=True)
                e = jnp.exp(s - top)
                total = colsum(e)
                LSEF[layer, h, p] = top + jnp.log(total)
                parts.append(dot(vt[h * 64 : (h + 1) * 64, :], e.astype(BF16)) / total)
            MXF[layer, :, p] = jnp.concatenate(parts, axis=0).T.astype(BF16).reshape(4, 64, 128)
            return carry

        lax.fori_loop(0, 4, pair, 0, unroll=True)

    def feature_backward(layer):
        zero = jnp.zeros((TOK, 128), BF16)

        def pair(p, carry):
            q, k, v = feature_parts(layer, p)
            up = upsend[:, p].reshape(TOK, 128)
            kt = turned(k)
            dqs, dks, dvs = [], [], []
            for h in range(2):
                mine = head_lanes((TOK, 128), h)
                s = dot_nt(jnp.where(mine, k, zero), q) + fmask_ref[...]
                probs = jnp.exp(s - LSEF[layer, h, p])
                dprobs = dot_nt(jnp.where(mine, v, zero), up)
                t = probs * dprobs
                ds = (t - probs * colsum(t)).astype(BF16)
                dvs.append(dot(probs.astype(BF16), up))
                dks.append(dot(ds, q))
                dqs.append(dot(kt[h * 64 : (h + 1) * 64, :], ds))
            first = head_lanes((TOK, 128), 0)
            dq = (jnp.concatenate(dqs, axis=0).T * SCALE).astype(BF16)
            dfeat[:, p, :, 0:128] = dq.reshape(4, 64, 128)
            dk = jnp.where(first, dks[0], dks[1]).astype(BF16)
            dfeat[:, p, :, 128:256] = dk.reshape(4, 64, 128)
            dv = jnp.where(first, dvs[0], dvs[1]).astype(BF16)
            dfeat[:, p, :, 256:384] = dv.reshape(4, 64, 128)
            return carry

        lax.fori_loop(0, 4, pair, 0, unroll=True)

    def outer_block(layer, g):
        return G[layer, g, :, :, :, :, OUTER : OUTER + 512].reshape(DIM, DIM)

    def gelu_parts(pre):
        inner = 0.7978845608028654 * (pre + 0.044715 * (pre * pre * pre))
        th = jnp.tanh(inner)
        return th

    def ff_forward(layer, last):
        ln_forward(layer, 2)
        dacc[...] = H[layer, 2] + vector(layer, 5)

        def cols(g, carry):
            pre = dot(A[layer, 2], weight_cols(layer, g, INNER, 512)) + VB[layer * VECS + 6 + g]
            act = (0.5 * pre * (1.0 + gelu_parts(pre))).astype(BF16)
            dacc[...] = dacc[...] + dot(act, outer_block(layer, g))
            return carry

        lax.fori_loop(0, 4, cols, 0, unroll=True)
        if last:
            hout_ref[...] = dacc[...]
        else:
            H[layer + 1, 0] = dacc[...]

    def round_gradient(layer, j, branch):
        down = g_ref[...].astype(BF16)
        DN[branch] = down
        put_vector(layer, j, colsum(down.astype(F32)))

    def add_up(g, part):
        @pl.when(g == 0)
        def _():
            dacc[...] = part

        @pl.when(g > 0)
        def _():
            dacc[...] = dacc[...] + part

    def ff_backward(layer):
        round_gradient(layer, 5, 2)

        def cols(g, carry):
            w1 = weight_cols(layer, g, INNER, 512)
            pre = dot(A[layer, 2], w1) + VB[layer * VECS + 6 + g]
            th = gelu_parts(pre)
            half = 0.5 * (1.0 + th)
            ACT[g] = (pre * half).astype(BF16)
            slope = half + 0.5 * pre * (1.0 - th * th) * (
                0.7978845608028654 * (1.0 + 3 * 0.044715 * (pre * pre))
            )
            dact = dot_nt(DN[2], outer_block(layer, g))
            dpre = (dact * slope).astype(BF16)
            DPRE[g] = dpre
            add_up(g, dot_nt(dpre, w1))
            row = colsum(dpre.astype(F32))
            for t in range(4):
                gsum[pl.ds((layer * VECS + 6 + g) * 4 + t, 1), :] = row[:, t * 128 : (t + 1) * 128]
            return carry

        lax.fori_loop(0, 4, cols, 0, unroll=True)
        ln_backward(layer, 2)

    def ff_weights(layer):
        at = turned(A[layer, 2])

        def cols(g, carry):
            DG(layer)[g, :, :, :, :, OUTER : OUTER + 512] = (
                dot(turned(ACT[g]), DN[2]).astype(BF16).reshape(2, 4, 4, 16, 512)
            )
            DG(layer)[:, :, :, g, :, INNER : INNER + 512] = (
                dot(at, DPRE[g]).astype(BF16).reshape(4, 2, 4, 16, 512)
            )
            return carry

        lax.fori_loop(0, 4, cols, 0, unroll=True)

    def attention_out_backward(layer, k):
        round_gradient(layer, 3 + k, k)
        up = dot_nt(DN[k], out_matrix(layer, k)).astype(BF16)
        for p in range(4):
            upsend[:, p] = up[:, p * 128 : (p + 1) * 128].reshape(4, 64, 128)

    def out_weights(layer, k, mx):
        dwo = dot(turned(join(mx)), DN[k]).astype(BF16)
        for g in range(4):
            DG(layer)[:, :, :, g, :, OUT[k] : OUT[k] + 128] = dwo[
                :, g * 128 : (g + 1) * 128
            ].reshape(4, 2, 4, 16, 128)

    def project_backward(layer, k, src):
        def cols(g, carry):
            w = weight_cols(layer, g, QKV[k], 384)
            add_up(g, dot_nt(src[:, g].reshape(TOK, 384), w))
            return carry

        lax.fori_loop(0, 4, cols, 0, unroll=True)
        ln_backward(layer, k)

    def project_weights(layer, k, src):
        at = turned(A[layer, k])

        def cols(g, carry):
            DG(layer)[:, :, :, g, :, QKV[k] : QKV[k] + 384] = (
                dot(at, src[:, g].reshape(TOK, 384)).astype(BF16).reshape(4, 2, 4, 16, 384)
            )
            return carry

        lax.fori_loop(0, 4, cols, 0, unroll=True)

    def rest(order, phase):
        return "".join(a for a in "zyx" if a not in order[:phase])

    def rs_copies(layer, group, phase):
        streams = RS_GROUPS[group]
        n = layer * 3 + group
        if phase == 0:
            cols = (streams[0][0], streams[2][1])
            src = held(DG(layer), dict(z=ALL, c=beside("c", 1)["c"], y=ALL, x=ALL), cols)
            dst = recvC.at[:, :, :, :, pl.ds(cols[0], cols[1] - cols[0])]
            return [remote(src, dst, rsc_s.at[n], rsc_r.at[n], beside("c", 1))]
        out = []
        for s, cols in enumerate(streams):
            order = RS_ORDERS[s]
            window = pl.ds(cols[0], cols[1] - cols[0])
            for d in (1, 2, 3):
                peer = beside(order[phase - 1], d)
                at = dict(z=ALL, c=me["c"], y=ALL, x=ALL)
                for axis in order[: phase - 1]:
                    at[axis] = me[axis]
                at[order[phase - 1]] = peer[order[phase - 1]]
                src = held(DG(layer), at, cols)
                if phase == 1:
                    dst = R1.at[d - 1, :, :, :, window]
                elif phase == 2:
                    dst = R2.at[layer, d - 1, :, :, window]
                else:
                    dst = R3.at[layer, d - 1, :, window]
                m = (phase - 1) * 3 + d - 1
                out.append(remote(src, dst, rs_s.at[n, s, m], rs_r.at[n, s, m], peer))
        return out

    def rs_sum(layer, group, phase):
        streams = RS_GROUPS[group]
        if phase == 0:
            first, last = streams[0][0], streams[2][1]

            def add(i, carry):
                z, y = lax.div(i, 4), lax.rem(i, 4)
                mine = DG(layer)[z, me["c"], y, :, :, first:last].astype(F32)
                other = recvC[z, y, :, :, first:last].astype(F32)
                DG(layer)[z, me["c"], y, :, :, first:last] = (mine + other).astype(BF16)
                return carry

            lax.fori_loop(0, 16, add, 0)
            return
        for s, (first, last) in enumerate(streams):
            order = RS_ORDERS[s]
            left = rest(order, phase)
            if phase == 1:

                def add(i, carry, left=left, order=order, first=first, last=last):
                    u = lax.div(i, 4)
                    v = lax.rem(i, 4)
                    at = {left[0]: u, left[1]: v, order[0]: me[order[0]]}
                    total = DG(layer)[at["z"], me["c"], at["y"], at["x"], :, first:last].astype(F32)
                    for d in range(3):
                        total = total + R1[d, u, v, :, first:last].astype(F32)
                    DG(layer)[at["z"], me["c"], at["y"], at["x"], :, first:last] = total.astype(BF16)
                    return carry

                lax.fori_loop(0, 16, add, 0)
            elif phase == 2:

                def add(u, carry, left=left, order=order, first=first, last=last):
                    at = dict(me)
                    at[left[0]] = u
                    total = DG(layer)[at["z"], me["c"], at["y"], at["x"], :, first:last].astype(F32)
                    for d in range(3):
                        total = total + R2[layer, d, u, :, first:last].astype(F32)
                    DG(layer)[at["z"], me["c"], at["y"], at["x"], :, first:last] = total.astype(BF16)
                    return carry

                lax.fori_loop(0, 4, add, 0)
            else:
                total = DG(layer)[me["z"], me["c"], me["y"], me["x"], :, first:last].astype(F32)
                for d in range(3):
                    total = total + R3[layer, d, :, first:last].astype(F32)
                fin[layer, :, first:last] = total

    def rs_step(layer, group, phase):
        if phase > 0:
            copies = rs_copies(layer, group, phase - 1)
            arrive(copies)
            leave(copies)
            rs_sum(layer, group, phase - 1)
        if phase < 4:
            start(rs_copies(layer, group, phase))

    start(x_copies())
    vsum[...] = vec_ref[...]
    start(vec_copies("x", vsum, vrecv, v_s, v_r, 0))
    xin[me["x"]] = blocks_ref[me["x"]]
    for layer in range(LAYERS):
        G[layer, me["z"], me["c"], me["y"], me["x"], :, OUTER : OUTER + 512] = outer_ref[layer]
    H[0, 0] = x_ref[...].astype(F32)
    row = lax.broadcasted_iota(jnp.int32, (64, 64), 0)
    col = lax.broadcasted_iota(jnp.int32, (64, 64), 1)

    def swap_groups(v):
        return (v & 3) | ((v & 12) << 2) | ((v & 48) >> 2)

    perm = jnp.where(swap_groups(row) == col, 1.0, 0.0).astype(BF16)
    arrive(x_copies())
    mixed_rows = dot(perm, xin[...].reshape(64, 768)).astype(BF16)
    for layer in range(LAYERS):
        for kk in range(4):
            G[layer, me["z"], me["c"], me["y"], me["x"], :, kk * 384 : (kk + 1) * 384] = mixed_rows[
                kk * 16 : (kk + 1) * 16, layer * 384 : (layer + 1) * 384
            ]
    ag_step(0, 0)

    def vec_sum(buf, recv, copies, slot, count):
        arrive(copies)
        leave(copies)
        total = buf[...].astype(F32)
        for d in range(count):
            total = total + recv[slot, d].astype(F32)
        buf[...] = total.astype(buf.dtype)

    vec_sum(vsum, vrecv, vec_copies("x", vsum, vrecv, v_s, v_r, 0), 0, 3)
    start(vec_copies("y", vsum, vrecv, v_s, v_r, 1))
    ag_step(0, 1)
    ag_step(1, 0)
    vec_sum(vsum, vrecv, vec_copies("y", vsum, vrecv, v_s, v_r, 1), 1, 3)
    start(vec_copies("z", vsum, vrecv, v_s, v_r, 2))
    ag_step(0, 2)
    ag_step(1, 1)
    vec_sum(vsum, vrecv, vec_copies("z", vsum, vrecv, v_s, v_r, 2), 2, 3)
    start(vec_copies("c", vsum, vrecv, v_s, v_r, 3))
    vec_sum(vsum, vrecv, vec_copies("c", vsum, vrecv, v_s, v_r, 3), 3, 1)
    vecs = vsum[...].astype(F32)
    for j in range(LAYERS * VECS):
        VB[j] = jnp.concatenate([vecs[4 * j + t : 4 * j + t + 1, :] for t in range(4)], axis=1)
    ag_step(0, 3)
    ln_forward(0, 0)
    ag_step(0, 4)

    def fsrc(y, x):
        return PK.at[y, x]

    def osrc(y, x):
        return osend.at[y * 4 + x]

    def usrc(y, x):
        return upsend.at[y, x]

    def dqsrc(y, x):
        return dqsend.at[y * 4 + x]

    def dsrc(y, x):
        return dsend.at[y * 4 + x]

    def to_column(n, src, dst):
        def then(step):
            def one(dy, carry):
                a2a_share(n, src, dst, dy, step)
                return carry

            lax.fori_loop(0, 4, one, 0)

        return then

    def to_row(n, src, dst):
        def then(step):
            def one(dx, carry):
                a2a_share(n, src, dst, step, dx)
                return carry

            lax.fori_loop(0, 4, one, 0)

        return then

    for layer in range(LAYERS):
        if layer > 0:
            ag_step(2, 3)
            ln_forward(layer, 0)
            ag_step(2, 4)
        qdst = QK.at[layer, fs]
        mdst = MX.at[layer, me["y"], me["x"]]
        project(layer, 0, PK, to_column(layer * 5, fsrc, qdst))
        if layer == 0:
            ag_step(1, 2)
        a2a_wait(layer * 5, fsrc, qdst)
        if layer == 0:
            ag_step(2, 0)
            ag_step(3, 0)
        else:
            ag_step(3, 3)
        sample_forward(layer, to_row(layer * 5 + 1, osrc, mdst))
        if layer == 0:
            ag_step(1, 3)
            ag_step(2, 1)
            ag_step(3, 1)
        else:
            ag_step(3, 4)
        a2a_wait(layer * 5 + 1, osrc, mdst)
        if layer == 0:
            ag_step(1, 4)
        attention_out(layer, 0, MX.at[layer])
        ln_forward(layer, 1)
        project(layer, 1, PKF.at[layer])
        if layer == 0:
            ag_step(2, 2)
            ag_step(3, 2)
        feature_forward(layer)
        attention_out(layer, 1, MXF.at[layer])
        ff_forward(layer, layer == LAYERS - 1)

    for group in range(len(AG_GROUPS)):
        for phase in range(4):
            leave(ag_copies(group, phase))
    g_ref[...] = seed_ref[...].astype(F32)
    for layer in (1, 0):
        udst = uprecv.at[layer, fs]
        dqdst = drecv.at[me["y"], me["x"], :, pl.ds(0, 128)]
        ddst = drecv.at[me["y"], me["x"], :, pl.ds(128, 256)]
        ff_backward(layer)
        if layer == 0:
            rs_step(1, 0, 3)
            rs_step(1, 1, 1)
            rs_step(1, 2, 0)
        attention_out_backward(layer, 1)
        feature_backward(layer)
        if layer == 0:
            rs_step(1, 0, 4)
            rs_step(1, 1, 2)
            rs_step(1, 2, 1)
        project_backward(layer, 1, dfeat)
        attention_out_backward(layer, 0)
        a2a_start(layer * 5 + 2, usrc, udst)
        ff_weights(layer)
        if layer == 0:
            rs_step(1, 1, 3)
            rs_step(1, 2, 2)
        rs_step(layer, 0, 0)
        a2a_wait(layer * 5 + 2, usrc, udst)
        sample_backward(layer, to_row(layer * 5 + 3, dqsrc, dqdst))
        a2a_start(layer * 5 + 4, dsrc, ddst)
        rs_step(layer, 0, 1)
        out_weights(layer, 0, MX.at[layer])
        out_weights(layer, 1, MXF.at[layer])
        project_weights(layer, 1, dfeat)
        rs_step(layer, 1, 0)
        if layer == 0:
            rs_step(1, 1, 4)
            rs_step(1, 2, 3)
        rs_step(layer, 0, 2)
        a2a_wait(layer * 5 + 3, dqsrc, dqdst)
        a2a_wait(layer * 5 + 4, dsrc, ddst)
        project_weights(layer, 0, drecv)
        if layer == 0:
            rs_step(0, 2, 0)
            rs_step(1, 2, 4)
            rs_step(0, 1, 1)
            rs_step(0, 0, 3)
        project_backward(layer, 0, drecv)
    gout_ref[...] = g_ref[...]

    gv = functools.partial(vec_copies, buf=gsum, recv=grecv, ss=gv_s, rs=gv_r)
    start(gv("x", slot=0))
    rs_step(0, 2, 1)
    rs_step(0, 1, 2)
    rs_step(0, 0, 4)
    vec_sum(gsum, grecv, gv("x", slot=0), 0, 3)
    start(gv("y", slot=1))
    rs_step(0, 2, 2)
    rs_step(0, 1, 3)
    vec_sum(gsum, grecv, gv("y", slot=1), 1, 3)
    start(gv("z", slot=2))
    rs_step(0, 2, 3)
    rs_step(0, 1, 4)
    vec_sum(gsum, grecv, gv("z", slot=2), 2, 3)
    start(gv("c", slot=3))
    rs_step(0, 2, 4)
    vec_sum(gsum, grecv, gv("c", slot=3), 3, 1)
    vecout_ref[...] = gsum[...]
    w2out_ref[...] = fin[:, :, OUTER : OUTER + 512]
    stacked = jnp.concatenate(
        [
            jnp.concatenate([fin[l, :, kk * 384 : (kk + 1) * 384] for l in range(LAYERS)], axis=1)
            for kk in range(4)
        ],
        axis=0,
    ).astype(BF16)
    xout[...] = dot(perm, stacked).astype(BF16).reshape(4, 16, 768)

    def xf_copies():
        return [
            remote(
                xout.at[beside("x", d)["x"]],
                xfin.at[me["x"]],
                xs_s.at[1, d - 1],
                xs_r.at[1, d - 1],
                beside("x", d),
            )
            for d in (1, 2, 3)
        ]

    start(xf_copies())
    xfin[me["x"]] = xout[me["x"]]
    arrive(xf_copies())
    wout_ref[...] = xfin[...].astype(F32)
    leave(xf_copies())
    leave(x_copies())


def vmem(shape, dtype):
    return pltpu.VMEM(shape, dtype)


def layers(x, seed, blocks, outer, vec, kmask, fmask):
    dma = pltpu.SemaphoreType.DMA
    whole = pl.BlockSpec(memory_space=pltpu.VMEM)
    return pl.pallas_call(
        kernel,
        out_shape=(
            jax.ShapeDtypeStruct((TOK, DIM), F32),
            jax.ShapeDtypeStruct((TOK, DIM), F32),
            jax.ShapeDtypeStruct((4, 16, 768), F32),
            jax.ShapeDtypeStruct((LAYERS, 16, 512), F32),
            jax.ShapeDtypeStruct((80, 128), F32),
        ),
        in_specs=[whole] * 7,
        out_specs=(whole,) * 5,
        scratch_shapes=[
            vmem((2, 4, 2, 4, 4, 16, 2048), BF16),
            vmem((4, 2, 4, 4, 16, 2048), BF16),
            vmem((4, 4, 4, 16, 2048), BF16),
            vmem((3, 4, 4, 16, 2048), BF16),
            vmem((2, 3, 4, 16, 2048), BF16),
            vmem((2, 3, 16, 2048), BF16),
            vmem((2, 16, 2048), F32),
            vmem((4, 16, 768), BF16),
            vmem((4, 16, 768), BF16),
            vmem((4, 16, 768), BF16),
            vmem((80, 128), BF16),
            vmem((4, 3, 80, 128), BF16),
            vmem((20, 1, 512), F32),
            vmem((80, 128), F32),
            vmem((4, 3, 80, 128), F32),
            vmem((2, 3, TOK, DIM), F32),
            vmem((4, 4, 64, 384), BF16),
            vmem((2, 16, 64, 384), BF16),
            vmem((2, 4, 4, 64, 384), BF16),
            vmem((2, 4, 4, 64, 128), BF16),
            vmem((2, 4, 4, 64, 128), BF16),
            vmem((2, 2, 4, 1, 256), F32),
            vmem((2, 2, 4, 1, 256), F32),
            vmem((16, 64, 128), BF16),
            vmem((4, 4, 64, 128), BF16),
            vmem((2, 16, 64, 128), BF16),
            vmem((16, 64, 128), BF16),
            vmem((16, 64, 256), BF16),
            vmem((4, 4, 64, 384), BF16),
            vmem((4, 4, 64, 384), BF16),
            vmem((2, 1024, 128), BF16),
            vmem((2, 1024, 128), BF16),
            vmem((128, 1024), BF16),
            vmem((2, 1024, 128), F32),
            vmem((2, 1024, 128), F32),
            vmem((2, 3, TOK, DIM), BF16),
            vmem((3, TOK, DIM), BF16),
            vmem((4, TOK, DIM), BF16),
            vmem((4, TOK, DIM), BF16),
            vmem((TOK, DIM), F32),
            vmem((TOK, DIM), F32),
            dma((10, 16)),
            dma((10, 16)),
            dma((4, 3, 9)),
            dma((4, 3, 9)),
            dma((4,)),
            dma((4,)),
            dma((6, 3, 9)),
            dma((6, 3, 9)),
            dma((6,)),
            dma((6,)),
            dma((2, 3)),
            dma((2, 3)),
            dma((4, 3)),
            dma((4, 3)),
            dma((4, 3)),
            dma((4, 3)),
        ],
        compiler_params=pltpu.CompilerParams(
            collective_id=0, has_side_effects=True, vmem_limit_bytes=63 * 2**20
        ),
    )(x, seed, blocks, outer, vec, kmask, fmask)


def body(
    entry_embeddings,
    norm_scales,
    triple_entry_matrix,
    mixing_exit_matrix,
    exit_bias,
    expanding_matrix,
    former_dense_bias,
    contracting_matrix,
    latter_dense_bias,
    row_presence_indicator,
    problem_column_number,
    loss_gradient,
):
    fs = lax.axis_index("fsdp")
    me = lax.axis_index("dp") * 16 + fs
    sample_ok = row_presence_indicator[0] > 0
    local_ok = lax.dynamic_slice_in_dim(sample_ok, fs * 64, 64)
    feature_ok = jnp.arange(4, dtype=jnp.int32) < problem_column_number[0]
    keep = feature_ok[:, None] & local_ok[None, :]

    x = entry_embeddings[0].transpose(1, 0, 2).reshape(TOK, DIM)
    seed = loss_gradient[0].transpose(1, 0, 2)
    seed = jnp.where(keep[:, :, None], seed, jnp.zeros_like(seed)).reshape(TOK, DIM)

    heads = triple_entry_matrix.reshape(2, 2, 4, 3, 4, 128)
    merge = mixing_exit_matrix.reshape(2, 2, 4, 1, 4, 128)
    chunks = jnp.concatenate([heads, merge], axis=3)
    chunks = chunks.transpose(4, 0, 2, 1, 3, 5).reshape(4, 2, 4, 8, 128)
    inner = expanding_matrix.reshape(2, 4, 4, 4, 128).transpose(2, 0, 1, 3, 4)
    chunks = jnp.concatenate([chunks, inner], axis=3).reshape(4, 2, 4, 4, 3, 128)
    blocks = chunks.transpose(0, 3, 2, 1, 4, 5).reshape(4, 16, 768)

    small = jnp.concatenate([norm_scales, exit_bias, latter_dense_bias[:, None]], axis=1)
    place = jnp.arange(512, dtype=jnp.int32) // 4 == me
    small = jnp.where(place, jnp.tile(small, (1, 1, 128)), 0).reshape(2, 24, 128)
    place = jnp.arange(2048, dtype=jnp.int32) // 16 == me
    large = jnp.where(place, jnp.tile(former_dense_bias, (1, 128)), 0).reshape(2, 16, 128)
    vec = jnp.concatenate([small, large], axis=1).reshape(80, 128).astype(BF16)

    kmask = jnp.where(sample_ok[:, None], 0.0, NEG).astype(BF16)
    kmask = jnp.broadcast_to(kmask, (1024, 128))
    key = jnp.arange(TOK, dtype=jnp.int32)
    same = (key[:, None] % 64 == key[None, :] % 64) & (key // 64 < problem_column_number[0])[:, None]
    fmask = jnp.where(same, 0.0, NEG).astype(F32)

    h, g, w, w2, vecs = layers(x, seed, blocks, contracting_matrix, vec, kmask, fmask)

    h = jnp.where(keep[:, :, None], h.reshape(4, 64, DIM), 0.0).transpose(1, 0, 2)
    g = g.reshape(4, 64, DIM).transpose(1, 0, 2)
    w = w.reshape(4, 4, 4, 2, 3, 128)
    w = w.transpose(3, 2, 1, 4, 0, 5).reshape(2, 4, 12, 4, 128)
    delta_heads = jnp.stack(
        [w[:, :, 0:3].reshape(2, 4, 1536), w[:, :, 4:7].reshape(2, 4, 1536)], axis=1
    )
    delta_merge = jnp.stack([w[:, :, 3].reshape(2, 4, 512), w[:, :, 7].reshape(2, 4, 512)], axis=1)
    delta_inner = w[:, :, 8:12].transpose(0, 1, 3, 2, 4).reshape(2, 4, 2048)
    vecs = vecs.reshape(2, 40 * 128)
    small = lax.dynamic_slice_in_dim(vecs[:, : 6 * 512].reshape(2, 6, 512), me * 4, 4, 2)
    thresholds = lax.dynamic_slice_in_dim(vecs[:, 6 * 512 :], me * 16, 16, 1)
    return (
        h[None],
        g[None],
        small[:, 0:3],
        delta_heads,
        delta_merge,
        small[:, 3:5],
        delta_inner,
        thresholds,
        w2,
        small[:, 5],
    )


def solution(mesh):
    both = ("dp", "fsdp")
    tokens = P("dp", "fsdp", None, None)
    weights = (
        P(None, None, both),
        P(None, None, both, None),
        P(None, None, both, None),
        P(None, None, both),
        P(None, both, None),
        P(None, both),
        P(None, both, None),
        P(None, both),
    )
    return jax.shard_map(
        body,
        mesh=mesh,
        in_specs=(tokens,) + weights + (P("dp", None), P("dp"), tokens),
        out_specs=(tokens, tokens) + weights,
        check_vma=False,
    )
```

```python
import functools

import jax
import jax.numpy as jnp
from jax import lax
from jax.experimental import pallas as pl
from jax.experimental.pallas import tpu as pltpu
from jax.sharding import PartitionSpec as P

EPS = 1e-05
NEG = -1e30
F32 = jnp.float32
BF16 = jnp.bfloat16
MESH = pl.DeviceIdType.MESH
LAYERS = 2
TOK = 256
DIM = 512
VECS = 10
SCALE = 0.125

QKV = (0, 512)
OUT = (384, 896)
INNER = 1024
OUTER = 1536

AG_ORDERS = ("xyz", "yzx", "zxy")
AG_GROUPS = (
    (0, ((0, 128), (128, 256), (256, 384))),
    (0, ((384, 1280), (1280, 1664), (1664, 2048))),
    (1, ((0, 128), (128, 256), (256, 384))),
    (1, ((384, 1280), (1280, 1664), (1664, 2048))),
)
RS_ORDERS = ("zyx", "xzy", "yxz")
RS_GROUPS = (
    ((1024, 1536), (1536, 1792), (1792, 2048)),
    ((384, 768), (768, 896), (896, 1024)),
    ((0, 128), (128, 256), (256, 384)),
)


def dot(a, b):
    return jnp.dot(a, b, preferred_element_type=F32)


def dot_nt(a, b):
    return lax.dot_general(a, b, (((1,), (1,)), ((), ())), preferred_element_type=F32)


def turned(a):
    return a.astype(F32).T.astype(BF16)


def colsum(a):
    return jnp.sum(a, axis=0, keepdims=True)


def lane(shape):
    return lax.broadcasted_iota(jnp.int32, shape, len(shape) - 1)


def kernel(
    entry_ref,
    gains_ref,
    heads_ref,
    merge_ref,
    offs_ref,
    inner_ref,
    thresh_ref,
    outer_ref,
    base_ref,
    present_ref,
    count_ref,
    loss_ref,
    hout_ref,
    gout_ref,
    wout_ref,
    w2out_ref,
    vecout_ref,
    keep_ref,
    G,
    dG,
    recvC,
    R1,
    R2,
    R3,
    fin,
    XB,
    xsend,
    xin,
    xout,
    xfin,
    vsum,
    vrecv,
    VP,
    VB,
    gsum,
    grecv,
    H,
    PK,
    QK,
    PKF,
    MX,
    MXF,
    LSE,
    LSEF,
    osend,
    upsend,
    uprecv,
    dqsend,
    dsend,
    drecv,
    dfeat,
    VALID,
    kmask,
    fmask,
    kh,
    vh,
    tr,
    DK,
    DV,
    A,
    DN,
    ACT,
    DPRE,
    dacc,
    g_ref,
    a2a_s,
    a2a_r,
    ag_s,
    ag_r,
    rs_s,
    rs_r,
    x_s,
    x_r,
    v_s,
    v_r,
):
    dp = lax.axis_index("dp")
    fs = lax.axis_index("fsdp")
    me = {"z": lax.div(dp, 2), "c": lax.rem(dp, 2), "y": lax.div(fs, 4), "x": lax.rem(fs, 4)}

    def device(at):
        return (at["z"] * 2 + at["c"], at["y"] * 4 + at["x"])

    def beside(axis, step):
        at = dict(me)
        at[axis] = lax.rem(me[axis] + step, 2 if axis == "c" else 4)
        return at

    def remote(src, dst, send, recv, at):
        return pltpu.make_async_remote_copy(
            src_ref=src,
            dst_ref=dst,
            send_sem=send,
            recv_sem=recv,
            device_id=device(at),
            device_id_type=MESH,
        )

    barrier = pltpu.get_barrier_semaphore()

    def greet(k, carry):
        at = dict(me)
        at["y"] = lax.rem(me["y"] + lax.div(k, 4), 4)
        at["x"] = lax.rem(me["x"] + lax.rem(k, 4), 4)
        pl.semaphore_signal(barrier, inc=1, device_id=device(at), device_id_type=MESH)
        return carry

    lax.fori_loop(1, 16, greet, 0)
    for step in (1, 2, 3):
        pl.semaphore_signal(barrier, inc=1, device_id=device(beside("z", step)), device_id_type=MESH)
    pl.semaphore_signal(barrier, inc=1, device_id=device(beside("c", 1)), device_id_type=MESH)
    pl.semaphore_wait(barrier, 19)

    def settle(ref, *sems):
        for sem in sems:
            pltpu.make_async_copy(ref, ref, sem).wait()

    def x_start(n, src, dst):
        for d in (1, 2, 3):
            at = beside("x", d)
            remote(src.at[at["x"]], dst.at[me["x"]], x_s.at[n], x_r.at[n], at).start()
        dst[me["x"]] = src[me["x"]]

    def vec_start(axis, n, buf, recv):
        for d in (1,) if axis == "c" else (1, 2, 3):
            remote(buf, recv.at[n % 4, d - 1], v_s.at[n], v_r.at[n], beside(axis, d)).start()

    def vec_sum(axis, n, buf, recv):
        count = 1 if axis == "c" else 3
        settle(recv.at[n % 4, pl.ds(0, count)], v_s.at[n], v_r.at[n])
        total = buf[...].astype(F32)
        for d in range(count):
            total = total + recv[n % 4, d].astype(F32)
        buf[...] = total.astype(buf.dtype)

    def held(ref, at, cols):
        return ref.at[at["z"], at["c"], at["y"], at["x"], :, pl.ds(cols[0], cols[1] - cols[0])]

    ALL = slice(None)

    def ag_start(group, phase):
        layer, streams = AG_GROUPS[group]
        sems = (ag_s.at[group, phase], ag_r.at[group, phase])
        if phase == 3:
            part = held(
                G.at[layer], dict(z=ALL, c=me["c"], y=ALL, x=ALL), (streams[0][0], streams[2][1])
            )
            remote(part, part, *sems, beside("c", 1)).start()
            return
        for s, cols in enumerate(streams):
            order = AG_ORDERS[s]
            at = dict(me)
            for axis in order[:phase]:
                at[axis] = ALL
            part = held(G.at[layer], at, cols)
            for d in (1, 2, 3):
                remote(part, part, *sems, beside(order[phase], d)).start()

    def ag_bytes(group, phase):
        layer, streams = AG_GROUPS[group]
        at = dict(z=pl.ds(0, 3), c=0, y=0, x=0)
        if phase == 3:
            at["z"] = ALL
        if phase >= 1:
            at["y"] = ALL
        if phase >= 2:
            at["x"] = ALL
        return held(G.at[layer], at, (streams[0][0], streams[2][1]))

    def ag_step(group, phase):
        if phase > 0:
            settle(ag_bytes(group, phase - 1), ag_r.at[group, phase - 1])
        if phase < 4:
            ag_start(group, phase)

    def plane(k):
        at = dict(me)
        at["y"] = lax.rem(me["y"] + lax.div(k, 4), 4)
        at["x"] = lax.rem(me["x"] + lax.rem(k, 4), 4)
        return at

    def a2a_one(n, k, src, dst):
        at = plane(k)
        return remote(src(at["y"], at["x"]), dst, a2a_s.at[n], a2a_r.at[n], at)

    def a2a_start(n, src, dst):
        def one(k, carry):
            a2a_one(n, k, src, dst).start()
            return carry

        lax.fori_loop(1, 16, one, 0)
        dst[...] = src(me["y"], me["x"])[...]

    def a2a_wait(n, blocks):
        settle(blocks.at[pl.ds(0, 15)], a2a_s.at[n], a2a_r.at[n])

    def a2a_share(n, src, dst, dy, dx):
        k = dy * 4 + dx

        @pl.when(k > 0)
        def _():
            a2a_one(n, k, src, dst).start()

        @pl.when(k == 0)
        def _():
            dst[...] = src(me["y"], me["x"])[...]

    def DG(layer):
        return dG if layer == 1 else G.at[1]

    def vector(layer, j):
        return VB[pl.ds(layer * VECS + j, 1), :]

    def ln_parts(v):
        mean = jnp.mean(v, axis=-1, keepdims=True)
        cen = v - mean
        r = lax.rsqrt(jnp.mean(cen * cen, axis=-1, keepdims=True) + EPS)
        return cen * r, r

    def ln_forward(layer, k):
        gain = vector(layer, k)

        def rows(i, carry):
            at = pl.ds(pl.multiple_of(i * 64, 64), 64)
            hat, unused = ln_parts(H[layer, k, at, :])
            A[layer, k, at, :] = (hat * gain).astype(BF16)
            return carry

        lax.fori_loop(0, 4, rows, 0, unroll=True)

    def ln_backward(layer, k):
        gain = vector(layer, k)

        def rows(i, total):
            at = pl.ds(pl.multiple_of(i * 64, 64), 64)
            hat, r = ln_parts(H[layer, k, at, :])
            dy = dacc[at, :]
            t = dy * gain
            back = r * (
                t
                - jnp.mean(t, axis=-1, keepdims=True)
                - hat * jnp.mean(t * hat, axis=-1, keepdims=True)
            )
            g_ref[at, :] = g_ref[at, :] + back
            return total + colsum(dy * hat)

        put_vector(layer, k, lax.fori_loop(0, 4, rows, jnp.zeros((1, DIM), F32), unroll=True))

    def put_vector(layer, j, row):
        gsum[pl.ds(layer * VECS + j, 1), :] = row

    def weight_cols(layer, g, first, width):
        return G[layer, :, :, :, g, :, first : first + width].reshape(DIM, width)

    def out_matrix(layer, k):
        return jnp.concatenate([weight_cols(layer, g, OUT[k], 128) for g in range(4)], axis=1)

    def project(layer, k, dst, then=None):
        def cols(step, carry):
            g = lax.rem(me["x"] + step, 4)
            out = dot(A[layer, k], weight_cols(layer, g, QKV[k], 384))
            dst[:, g] = out.astype(BF16).reshape(4, 64, 384)
            if then is not None:
                then(step)
            return carry

        lax.fori_loop(0, 4, cols, 0, unroll=True)

    def join(mx):
        return jnp.concatenate([mx[:, p].reshape(TOK, 128) for p in range(4)], axis=1)

    def attention_out(layer, k, mx):
        H[layer, k + 1] = (
            H[layer, k] + dot(join(mx), out_matrix(layer, k)) + vector(layer, 3 + k)
        )

    def head_lanes(shape, h):
        where = lane(shape)
        return (where >= h * 64) & (where < (h + 1) * 64)

    def sample_prepare(layer, backward):
        k = QK[layer, :, :, 128:256].reshape(1024, 128)
        v = QK[layer, :, :, 256:384].reshape(1024, 128)
        where = lane((1024, 128))
        zero = jnp.zeros((1024, 128), BF16)
        for h in range(2):
            mine = head_lanes((1024, 128), h)
            kh[h] = jnp.where(mine, k, jnp.where(where == 64 * (1 - h), kmask[...], zero))
            if backward:
                vh[h] = jnp.where(mine, v, zero)
        tr[...] = turned(k if backward else v)

    def sample_query(layer, i):
        return QK[layer, pl.ds(i * 4, 4), :, 0:128].reshape(256, 128) * jnp.asarray(SCALE, BF16)

    def with_one(q, h):
        return jnp.where(lane((256, 128)) == 64 * (1 - h), jnp.ones((256, 128), BF16), q)

    def sample_forward(layer, then):
        sample_prepare(layer, False)

        def block(step, carry):
            i = lax.rem(me["y"] + step, 4)
            q = sample_query(layer, i)
            parts = []
            for h in range(2):
                s = dot_nt(kh[h], with_one(q, h))
                top = jnp.max(s, axis=0, keepdims=True)
                e = jnp.exp(s - top)
                total = colsum(e)
                LSE[layer, h, i] = top + jnp.log(total)
                parts.append(dot(tr[h * 64 : (h + 1) * 64, :], e.astype(BF16)) / total)
            mixed = jnp.concatenate(parts, axis=0).T.astype(BF16)
            osend[pl.ds(i * 4, 4)] = mixed.reshape(4, 64, 128)
            then(step)
            return carry

        lax.fori_loop(0, 4, block, 0, unroll=True)

    def sample_backward(layer, then):
        sample_prepare(layer, True)

        def block(step, carry):
            i = lax.rem(me["y"] + step, 4)
            q = sample_query(layer, i)
            up = uprecv[layer, pl.ds(i * 4, 4)].reshape(256, 128)
            parts = []
            for h in range(2):
                s = dot_nt(kh[h], with_one(q, h))
                p = jnp.exp(s - LSE[layer, h, i])
                dprobs = dot_nt(vh[h], up)
                t = p * dprobs
                ds = (t - p * colsum(t)).astype(BF16)
                dv = dot(p.astype(BF16), up)
                dk = dot(ds, q)

                @pl.when(step == 0)
                def _():
                    DV[h] = dv
                    DK[h] = dk

                @pl.when(step > 0)
                def _():
                    DV[h] = DV[h] + dv
                    DK[h] = DK[h] + dk

                parts.append(dot(tr[h * 64 : (h + 1) * 64, :], ds))
            dq = (jnp.concatenate(parts, axis=0).T * SCALE).astype(BF16)
            dqsend[pl.ds(i * 4, 4)] = dq.reshape(4, 64, 128)
            then(step)
            return carry

        lax.fori_loop(0, 4, block, 0, unroll=True)
        first = head_lanes((1024, 128), 0)
        dsend[:, :, 0:128] = jnp.where(first, DK[0], DK[1]).astype(BF16).reshape(16, 64, 128)
        dsend[:, :, 128:256] = jnp.where(first, DV[0], DV[1]).astype(BF16).reshape(16, 64, 128)

    def feature_parts(layer, p):
        q = PKF[layer, :, p, :, 0:128].reshape(TOK, 128) * jnp.asarray(SCALE, BF16)
        k = PKF[layer, :, p, :, 128:256].reshape(TOK, 128)
        v = PKF[layer, :, p, :, 256:384].reshape(TOK, 128)
        return q, k, v

    def feature_forward(layer):
        zero = jnp.zeros((TOK, 128), BF16)

        def pair(p, carry):
            q, k, v = feature_parts(layer, p)
            vt = turned(v)
            parts = []
            for h in range(2):
                mine = head_lanes((TOK, 128), h)
                s = dot_nt(jnp.where(mine, k, zero), q) + fmask[...]
                top = jnp.max(s, axis=0, keepdims=True)
                e = jnp.exp(s - top)
                total = colsum(e)
                LSEF[layer, h, p] = top + jnp.log(total)
                parts.append(dot(vt[h * 64 : (h + 1) * 64, :], e.astype(BF16)) / total)
            MXF[layer, :, p] = jnp.concatenate(parts, axis=0).T.astype(BF16).reshape(4, 64, 128)
            return carry

        lax.fori_loop(0, 4, pair, 0, unroll=True)

    def feature_backward(layer):
        zero = jnp.zeros((TOK, 128), BF16)

        def pair(p, carry):
            q, k, v = feature_parts(layer, p)
            up = upsend[:, p].reshape(TOK, 128)
            kt = turned(k)
            dqs, dks, dvs = [], [], []
            for h in range(2):
                mine = head_lanes((TOK, 128), h)
                s = dot_nt(jnp.where(mine, k, zero), q) + fmask[...]
                probs = jnp.exp(s - LSEF[layer, h, p])
                dprobs = dot_nt(jnp.where(mine, v, zero), up)
                t = probs * dprobs
                ds = (t - probs * colsum(t)).astype(BF16)
                dvs.append(dot(probs.astype(BF16), up))
                dks.append(dot(ds, q))
                dqs.append(dot(kt[h * 64 : (h + 1) * 64, :], ds))
            first = head_lanes((TOK, 128), 0)
            dq = (jnp.concatenate(dqs, axis=0).T * SCALE).astype(BF16)
            dfeat[:, p, :, 0:128] = dq.reshape(4, 64, 128)
            dk = jnp.where(first, dks[0], dks[1]).astype(BF16)
            dfeat[:, p, :, 128:256] = dk.reshape(4, 64, 128)
            dv = jnp.where(first, dvs[0], dvs[1]).astype(BF16)
            dfeat[:, p, :, 256:384] = dv.reshape(4, 64, 128)
            return carry

        lax.fori_loop(0, 4, pair, 0, unroll=True)

    def outer_block(layer, g):
        return G[layer, g, :, :, :, :, OUTER : OUTER + 512].reshape(DIM, DIM)

    def gelu_parts(pre):
        inner = 0.7978845608028654 * (pre + 0.044715 * (pre * pre * pre))
        th = jnp.tanh(inner)
        return th

    def ff_forward(layer, last):
        ln_forward(layer, 2)
        dacc[...] = H[layer, 2] + vector(layer, 5)

        def cols(g, carry):
            pre = dot(A[layer, 2], weight_cols(layer, g, INNER, 512)) + vector(layer, 6 + g)
            act = (0.5 * pre * (1.0 + gelu_parts(pre))).astype(BF16)
            dacc[...] = dacc[...] + dot(act, outer_block(layer, g))
            return carry

        lax.fori_loop(0, 4, cols, 0, unroll=True)
        if last:
            hout_ref[...] = dacc[...]
        else:
            H[layer + 1, 0] = dacc[...]

    def round_gradient(layer, j, branch):
        down = g_ref[...].astype(BF16)
        DN[branch] = down
        put_vector(layer, j, colsum(down.astype(F32)))

    def add_up(g, part):
        @pl.when(g == 0)
        def _():
            dacc[...] = part

        @pl.when(g > 0)
        def _():
            dacc[...] = dacc[...] + part

    def ff_backward(layer):
        round_gradient(layer, 5, 2)

        def cols(g, carry):
            w1 = weight_cols(layer, g, INNER, 512)
            pre = dot(A[layer, 2], w1) + vector(layer, 6 + g)
            th = gelu_parts(pre)
            half = 0.5 * (1.0 + th)
            ACT[g] = (pre * half).astype(BF16)
            slope = half + 0.5 * pre * (1.0 - th * th) * (
                0.7978845608028654 * (1.0 + 3 * 0.044715 * (pre * pre))
            )
            dact = dot_nt(DN[2], outer_block(layer, g))
            dpre = (dact * slope).astype(BF16)
            DPRE[g] = dpre
            add_up(g, dot_nt(dpre, w1))
            row = colsum(dpre.astype(F32))
            put_vector(layer, 6 + g, row)
            return carry

        lax.fori_loop(0, 4, cols, 0, unroll=True)
        ln_backward(layer, 2)

    def ff_weights(layer):
        at = turned(A[layer, 2])

        def cols(g, carry):
            DG(layer)[g, :, :, :, :, OUTER : OUTER + 512] = (
                dot(turned(ACT[g]), DN[2]).astype(BF16).reshape(2, 4, 4, 16, 512)
            )
            DG(layer)[:, :, :, g, :, INNER : INNER + 512] = (
                dot(at, DPRE[g]).astype(BF16).reshape(4, 2, 4, 16, 512)
            )
            return carry

        lax.fori_loop(0, 4, cols, 0, unroll=True)

    def attention_out_backward(layer, k):
        round_gradient(layer, 3 + k, k)
        up = dot_nt(DN[k], out_matrix(layer, k)).astype(BF16)
        for p in range(4):
            upsend[:, p] = up[:, p * 128 : (p + 1) * 128].reshape(4, 64, 128)

    def out_weights(layer, k, mx):
        dwo = dot(turned(join(mx)), DN[k]).astype(BF16)
        for g in range(4):
            DG(layer)[:, :, :, g, :, OUT[k] : OUT[k] + 128] = dwo[
                :, g * 128 : (g + 1) * 128
            ].reshape(4, 2, 4, 16, 128)

    def project_backward(layer, k, src):
        def cols(g, carry):
            w = weight_cols(layer, g, QKV[k], 384)
            add_up(g, dot_nt(src[:, g].reshape(TOK, 384), w))
            return carry

        lax.fori_loop(0, 4, cols, 0, unroll=True)
        ln_backward(layer, k)

    def project_weights(layer, k, src):
        at = turned(A[layer, k])

        def cols(g, carry):
            DG(layer)[:, :, :, g, :, QKV[k] : QKV[k] + 384] = (
                dot(at, src[:, g].reshape(TOK, 384)).astype(BF16).reshape(4, 2, 4, 16, 384)
            )
            return carry

        lax.fori_loop(0, 4, cols, 0, unroll=True)

    def rest(order, phase):
        return "".join(a for a in "zyx" if a not in order[:phase])

    def rs_start(layer, group, phase):
        streams = RS_GROUPS[group]
        sems = (rs_s.at[layer * 3 + group, phase], rs_r.at[layer * 3 + group, phase])
        if phase == 0:
            cols = (streams[0][0], streams[2][1])
            src = held(DG(layer), dict(z=ALL, c=beside("c", 1)["c"], y=ALL, x=ALL), cols)
            remote(src, rs_landing(layer, group, 0), *sems, beside("c", 1)).start()
            return
        for s, cols in enumerate(streams):
            order = RS_ORDERS[s]
            window = pl.ds(cols[0], cols[1] - cols[0])
            axis = order[phase - 1]
            for d in (1, 2, 3):
                peer = beside(axis, d)
                at = dict(z=ALL, c=me["c"], y=ALL, x=ALL)
                for before in order[: phase - 1]:
                    at[before] = me[before]
                at[axis] = peer[axis]
                if phase == 1:
                    dst = R1.at[d - 1, :, :, :, window]
                elif phase == 2:
                    dst = R2.at[layer, d - 1, :, :, window]
                else:
                    dst = R3.at[layer, d - 1, :, window]
                remote(held(DG(layer), at, cols), dst, *sems, peer).start()

    def rs_landing(layer, group, phase):
        streams = RS_GROUPS[group]
        window = pl.ds(streams[0][0], streams[2][1] - streams[0][0])
        if phase == 0:
            return recvC.at[:, :, :, :, window]
        if phase == 1:
            return R1.at[:, :, :, :, window]
        if phase == 2:
            return R2.at[layer, :, :, :, window]
        return R3.at[layer, :, :, window]

    def rs_sum(layer, group, phase):
        streams = RS_GROUPS[group]
        if phase == 0:
            first, last = streams[0][0], streams[2][1]

            def add(i, carry):
                z, y = lax.div(i, 4), lax.rem(i, 4)
                mine = DG(layer)[z, me["c"], y, :, :, first:last].astype(F32)
                other = recvC[z, y, :, :, first:last].astype(F32)
                DG(layer)[z, me["c"], y, :, :, first:last] = (mine + other).astype(BF16)
                return carry

            lax.fori_loop(0, 16, add, 0)
            return
        for s, (first, last) in enumerate(streams):
            order = RS_ORDERS[s]
            left = rest(order, phase)
            if phase == 1:

                def add(i, carry, left=left, order=order, first=first, last=last):
                    u = lax.div(i, 4)
                    v = lax.rem(i, 4)
                    at = {left[0]: u, left[1]: v, order[0]: me[order[0]]}
                    total = DG(layer)[at["z"], me["c"], at["y"], at["x"], :, first:last].astype(F32)
                    for d in range(3):
                        total = total + R1[d, u, v, :, first:last].astype(F32)
                    DG(layer)[at["z"], me["c"], at["y"], at["x"], :, first:last] = total.astype(BF16)
                    return carry

                lax.fori_loop(0, 16, add, 0)
            elif phase == 2:

                def add(u, carry, left=left, order=order, first=first, last=last):
                    at = dict(me)
                    at[left[0]] = u
                    total = DG(layer)[at["z"], me["c"], at["y"], at["x"], :, first:last].astype(F32)
                    for d in range(3):
                        total = total + R2[layer, d, u, :, first:last].astype(F32)
                    DG(layer)[at["z"], me["c"], at["y"], at["x"], :, first:last] = total.astype(BF16)
                    return carry

                lax.fori_loop(0, 4, add, 0)
            else:
                total = DG(layer)[me["z"], me["c"], me["y"], me["x"], :, first:last].astype(F32)
                for d in range(3):
                    total = total + R3[layer, d, :, first:last].astype(F32)
                fin[layer, :, first:last] = total

    def rs_step(layer, group, phase):
        if phase > 0:
            n = layer * 3 + group
            settle(rs_landing(layer, group, phase - 1), rs_s.at[n, phase - 1], rs_r.at[n, phase - 1])
            rs_sum(layer, group, phase - 1)
        if phase < 4:
            rs_start(layer, group, phase)

    for layer in range(LAYERS):
        for g in range(4):

            def cols(ref, at, first, width=128):
                return ref[at + (slice(None), slice(first, first + width))].astype(F32)

            heads = [
                [cols(heads_ref, (layer, k), t * 512 + g * 128) for t in range(3)] for k in range(2)
            ]
            merge = [cols(merge_ref, (layer, k), g * 128) for k in range(2)]
            inner = [cols(inner_ref, (layer,), g * 512 + t * 128) for t in range(4)]
            chunks = heads[0] + merge[:1] + heads[1] + merge[1:] + inner
            for q, chunk in enumerate(chunks):
                kk, gg = q // 3, q % 3
                first = layer * 384 + gg * 128
                XB[g, kk * 4 : kk * 4 + 4, first : first + 128] = chunk
    xsend[...] = XB[...].astype(BF16)
    x_start(0, xsend, xin)

    where = lax.broadcasted_iota(jnp.int32, (1, DIM), 1)
    number = dp * 16 + fs

    def spread(v, width, t):
        out = jnp.zeros((v.shape[0], DIM), F32)
        for r in range(width):
            here = where + t * DIM == number * width + r
            out = jnp.where(here, v[:, r : r + 1], out)
        return out

    VP[...] = jnp.zeros_like(VP)
    gsum[...] = jnp.zeros_like(gsum)
    for layer in range(LAYERS):
        at = layer * VECS
        VP[at : at + 3, :] = spread(gains_ref[layer].astype(F32), 4, 0)
        VP[at + 3 : at + 5, :] = spread(offs_ref[layer].astype(F32), 4, 0)
        VP[at + 5 : at + 6, :] = spread(base_ref[layer : layer + 1, :].astype(F32), 4, 0)
        for t in range(4):
            VP[at + 6 + t : at + 7 + t, :] = spread(
                thresh_ref[layer : layer + 1, :].astype(F32), 16, t
            )
    vsum[...] = VP[...].astype(BF16)
    vec_start("x", 0, vsum, vrecv)
    for layer in range(LAYERS):
        G[layer, me["z"], me["c"], me["y"], me["x"], :, OUTER : OUTER + 512] = outer_ref[layer]
    row = lax.broadcasted_iota(jnp.int32, (64, 64), 0)
    col = lax.broadcasted_iota(jnp.int32, (64, 64), 1)

    def swap_groups(v):
        return (v & 3) | ((v & 12) << 2) | ((v & 48) >> 2)

    perm = jnp.where(swap_groups(row) == col, 1.0, 0.0).astype(BF16)
    settle(xin.at[pl.ds(0, 3)], x_r.at[0])
    mixed_rows = dot(perm, xin[...].reshape(64, 768)).astype(BF16)
    for layer in range(LAYERS):
        for kk in range(4):
            G[layer, me["z"], me["c"], me["y"], me["x"], :, kk * 384 : (kk + 1) * 384] = mixed_rows[
                kk * 16 : (kk + 1) * 16, layer * 384 : (layer + 1) * 384
            ]
    ag_step(0, 0)
    for f in range(4):
        H[0, 0, f * 64 : (f + 1) * 64, :] = entry_ref[:, f, :].astype(F32)
    vec_sum("x", 0, vsum, vrecv)
    vec_start("y", 1, vsum, vrecv)
    ag_step(0, 1)
    ag_step(1, 0)
    VALID[...] = jnp.broadcast_to(present_ref[...].astype(F32), (128, 1024)).T
    kmask[...] = jnp.where(VALID[...] > 0.0, 0.0, NEG).astype(BF16)
    keep_ref[...] = VALID[pl.ds(pl.multiple_of(fs * 64, 64), 64), :]
    vec_sum("y", 1, vsum, vrecv)
    vec_start("z", 2, vsum, vrecv)
    ag_step(0, 2)
    ag_step(1, 1)
    key = lax.broadcasted_iota(jnp.int32, (TOK, TOK), 0)
    query = lax.broadcasted_iota(jnp.int32, (TOK, TOK), 1)
    same = ((key & 63) == (query & 63)) & ((key >> 6) < count_ref[...])
    fmask[...] = jnp.where(same, 0.0, NEG)
    vec_sum("z", 2, vsum, vrecv)
    vec_start("c", 3, vsum, vrecv)
    ag_step(0, 3)
    vec_sum("c", 3, vsum, vrecv)
    VB[...] = vsum[...].astype(F32)
    ln_forward(0, 0)
    ag_step(0, 4)

    def fsrc(y, x):
        return PK.at[y, x]

    def osrc(y, x):
        return osend.at[y * 4 + x]

    def usrc(y, x):
        return upsend.at[y, x]

    def dqsrc(y, x):
        return dqsend.at[y * 4 + x]

    def dsrc(y, x):
        return dsend.at[y * 4 + x]

    def to_column(n, src, dst):
        def then(step):
            def one(dy, carry):
                a2a_share(n, src, dst, dy, step)
                return carry

            lax.fori_loop(0, 4, one, 0)

        return then

    def to_row(n, src, dst):
        def then(step):
            def one(dx, carry):
                a2a_share(n, src, dst, step, dx)
                return carry

            lax.fori_loop(0, 4, one, 0)

        return then

    for layer in range(LAYERS):
        if layer > 0:
            ag_step(2, 3)
            ln_forward(layer, 0)
            ag_step(2, 4)
        qdst = QK.at[layer, fs]
        mdst = MX.at[layer, me["y"], me["x"]]
        project(layer, 0, PK, to_column(layer * 5, fsrc, qdst))
        if layer == 0:
            ag_step(1, 2)
        a2a_wait(layer * 5, QK.at[layer])
        if layer == 0:
            ag_step(2, 0)
            ag_step(3, 0)
        else:
            ag_step(3, 3)
        sample_forward(layer, to_row(layer * 5 + 1, osrc, mdst))
        if layer == 0:
            ag_step(1, 3)
            ag_step(2, 1)
            ag_step(3, 1)
        else:
            ag_step(3, 4)
        a2a_wait(layer * 5 + 1, osend)
        if layer == 0:
            ag_step(1, 4)
        attention_out(layer, 0, MX.at[layer])
        ln_forward(layer, 1)
        project(layer, 1, PKF.at[layer])
        if layer == 0:
            ag_step(2, 2)
            ag_step(3, 2)
        feature_forward(layer)
        attention_out(layer, 1, MXF.at[layer])
        ff_forward(layer, layer == LAYERS - 1)

    for group in range(len(AG_GROUPS)):
        for phase in range(4):
            settle(ag_bytes(group, phase), ag_s.at[group, phase])
    valid = keep_ref[:, 0:1] > 0.0
    for f in range(4):
        real = valid & (count_ref[...] > f)
        g_ref[f * 64 : (f + 1) * 64, :] = jnp.where(real, loss_ref[:, f, :].astype(F32), 0.0)
    for layer in (1, 0):
        udst = uprecv.at[layer, fs]
        dqdst = drecv.at[me["y"], me["x"], :, pl.ds(0, 128)]
        ddst = drecv.at[me["y"], me["x"], :, pl.ds(128, 256)]
        ff_backward(layer)
        ff_weights(layer)
        if layer == 0:
            rs_step(1, 2, 1)
        rs_step(layer, 0, 0)
        if layer == 0:
            rs_step(1, 0, 4)
        attention_out_backward(layer, 1)
        feature_backward(layer)
        if layer == 0:
            rs_step(1, 1, 3)
            rs_step(1, 2, 2)
        project_backward(layer, 1, dfeat)
        attention_out_backward(layer, 0)
        a2a_start(layer * 5 + 2, usrc, udst)
        rs_step(layer, 0, 1)
        out_weights(layer, 1, MXF.at[layer])
        project_weights(layer, 1, dfeat)
        out_weights(layer, 0, MX.at[layer])
        rs_step(layer, 1, 0)
        if layer == 0:
            rs_step(1, 2, 3)
            rs_step(1, 1, 4)
        a2a_wait(layer * 5 + 2, uprecv.at[layer])
        sample_backward(layer, to_row(layer * 5 + 3, dqsrc, dqdst))
        a2a_start(layer * 5 + 4, dsrc, ddst)
        rs_step(layer, 0, 2)
        rs_step(layer, 1, 1)
        if layer == 0:
            rs_step(1, 2, 4)
        a2a_wait(layer * 5 + 3, dqsend)
        a2a_wait(layer * 5 + 4, dsend)
        project_weights(layer, 0, drecv)
        rs_step(layer, 2, 0)
        project_backward(layer, 0, drecv)
        rs_step(layer, 0, 3)
        rs_step(layer, 1, 2)
    gout_ref[...] = g_ref[...]

    vec_start("x", 4, gsum, grecv)
    rs_step(0, 2, 1)
    rs_step(0, 0, 4)
    vec_sum("x", 4, gsum, grecv)
    vec_start("y", 5, gsum, grecv)
    rs_step(0, 1, 3)
    rs_step(0, 2, 2)
    vec_sum("y", 5, gsum, grecv)
    vec_start("z", 6, gsum, grecv)
    rs_step(0, 1, 4)
    rs_step(0, 2, 3)
    vec_sum("z", 6, gsum, grecv)
    vec_start("c", 7, gsum, grecv)
    rs_step(0, 2, 4)
    w2out_ref[...] = fin[:, :, OUTER : OUTER + 512]
    stacked = jnp.concatenate(
        [
            jnp.concatenate([fin[l, :, kk * 384 : (kk + 1) * 384] for l in range(LAYERS)], axis=1)
            for kk in range(4)
        ],
        axis=0,
    ).astype(BF16)
    xout[...] = dot(perm, stacked).astype(BF16).reshape(4, 16, 768)
    x_start(1, xout, xfin)
    vec_sum("c", 7, gsum, grecv)
    at = lax.broadcasted_iota(jnp.int32, (DIM, 128), 0)
    to = lax.broadcasted_iota(jnp.int32, (DIM, 128), 1)
    exact = lax.Precision.HIGHEST
    few = jnp.where((at == number * 4 + to) & (to < 4), 1.0, 0.0)
    many = jnp.where((at == lax.rem(number, 32) * 16 + to) & (to < 16), 1.0, 0.0)
    few = jnp.dot(gsum[...], few, precision=exact, preferred_element_type=F32)
    many = jnp.dot(gsum[...], many, precision=exact, preferred_element_type=F32)
    vecout_ref[0:24, :] = few
    for layer in range(LAYERS):
        first = layer * VECS + 6
        line = jnp.zeros((1, 128), F32)
        for t in range(4):
            line = line + jnp.where(lax.div(number, 32) == t, many[first + t : first + t + 1], 0.0)
        vecout_ref[24 + layer : 25 + layer, :] = line
    settle(xfin.at[pl.ds(0, 3)], x_s.at[1], x_r.at[1])
    wout_ref[...] = xfin[...].astype(F32)
    settle(xin.at[pl.ds(0, 3)], x_s.at[0])


def write_outputs(
    h_ref,
    g_ref,
    w_ref,
    w2_ref,
    vec_ref,
    keep_ref,
    count_ref,
    act_out,
    tokens_out,
    gains_out,
    heads_out,
    merge_out,
    offs_out,
    inner_out,
    thresh_out,
    outer_out,
    base_out,
):
    valid = keep_ref[:, 0:1] > 0.0
    for f in range(4):
        rows = slice(f * 64, (f + 1) * 64)
        act_out[0, :, f, :] = jnp.where(valid & (count_ref[...] > f), h_ref[rows, :], 0.0)
        tokens_out[0, :, f, :] = g_ref[rows, :]
    for layer in range(LAYERS):
        for g in range(4):
            for q in range(12):
                kk, gg = q // 3, q % 3
                first = layer * 384 + gg * 128
                chunk = w_ref[g, kk * 4 : kk * 4 + 4, first : first + 128]
                if q in (3, 7):
                    merge_out[layer, q // 4, :, g * 128 : (g + 1) * 128] = chunk
                elif q < 8:
                    to = (q % 4) * 512 + g * 128
                    heads_out[layer, q // 4, :, to : to + 128] = chunk
                else:
                    to = g * 512 + (q - 8) * 128
                    inner_out[layer, :, to : to + 128] = chunk
        at = layer * VECS
        gains_out[layer] = vec_ref[at : at + 3, 0:4]
        offs_out[layer] = vec_ref[at + 3 : at + 5, 0:4]
        base_out[layer : layer + 1, :] = vec_ref[at + 5 : at + 6, 0:4]
        thresh_out[layer : layer + 1, :] = vec_ref[24 + layer : 25 + layer, 0:16]
    outer_out[...] = w2_ref[...]


def vmem(shape, dtype):
    return pltpu.VMEM(shape, dtype)


def layers(*arrays):
    dma = pltpu.SemaphoreType.DMA
    whole = pl.BlockSpec(memory_space=pltpu.VMEM)
    return pl.pallas_call(
        kernel,
        out_shape=(
            jax.ShapeDtypeStruct((TOK, DIM), F32),
            jax.ShapeDtypeStruct((TOK, DIM), F32),
            jax.ShapeDtypeStruct((4, 16, 768), F32),
            jax.ShapeDtypeStruct((LAYERS, 16, 512), F32),
            jax.ShapeDtypeStruct((32, 128), F32),
            jax.ShapeDtypeStruct((64, 128), F32),
        ),
        in_specs=[whole] * 12,
        out_specs=(whole,) * 6,
        scratch_shapes=[
            vmem((2, 4, 2, 4, 4, 16, 2048), BF16),
            vmem((4, 2, 4, 4, 16, 2048), BF16),
            vmem((4, 4, 4, 16, 2048), BF16),
            vmem((3, 4, 4, 16, 2048), BF16),
            vmem((2, 3, 4, 16, 2048), BF16),
            vmem((2, 3, 16, 2048), BF16),
            vmem((2, 16, 2048), F32),
            vmem((4, 16, 768), F32),
            vmem((4, 16, 768), BF16),
            vmem((4, 16, 768), BF16),
            vmem((4, 16, 768), BF16),
            vmem((4, 16, 768), BF16),
            vmem((32, 512), BF16),
            vmem((4, 3, 32, 512), BF16),
            vmem((32, 512), F32),
            vmem((32, 512), F32),
            vmem((24, 512), F32),
            vmem((4, 3, 24, 512), F32),
            vmem((2, 3, TOK, DIM), F32),
            vmem((4, 4, 64, 384), BF16),
            vmem((2, 16, 64, 384), BF16),
            vmem((2, 4, 4, 64, 384), BF16),
            vmem((2, 4, 4, 64, 128), BF16),
            vmem((2, 4, 4, 64, 128), BF16),
            vmem((2, 2, 4, 1, 256), F32),
            vmem((2, 2, 4, 1, 256), F32),
            vmem((16, 64, 128), BF16),
            vmem((4, 4, 64, 128), BF16),
            vmem((2, 16, 64, 128), BF16),
            vmem((16, 64, 128), BF16),
            vmem((16, 64, 256), BF16),
            vmem((4, 4, 64, 384), BF16),
            vmem((4, 4, 64, 384), BF16),
            vmem((1024, 128), F32),
            vmem((1024, 128), BF16),
            vmem((TOK, TOK), F32),
            vmem((2, 1024, 128), BF16),
            vmem((2, 1024, 128), BF16),
            vmem((128, 1024), BF16),
            vmem((2, 1024, 128), F32),
            vmem((2, 1024, 128), F32),
            vmem((2, 3, TOK, DIM), BF16),
            vmem((3, TOK, DIM), BF16),
            vmem((4, TOK, DIM), BF16),
            vmem((4, TOK, DIM), BF16),
            vmem((TOK, DIM), F32),
            vmem((TOK, DIM), F32),
            dma((10,)),
            dma((10,)),
            dma((4, 4)),
            dma((4, 4)),
            dma((6, 4)),
            dma((6, 4)),
            dma((2,)),
            dma((2,)),
            dma((8,)),
            dma((8,)),
        ],
        compiler_params=pltpu.CompilerParams(
            collective_id=0, has_side_effects=True, vmem_limit_bytes=63 * 2**20
        ),
    )(*arrays)


def outputs(*arrays):
    whole = pl.BlockSpec(memory_space=pltpu.VMEM)
    shapes = (
        (1, 64, 4, 512),
        (1, 64, 4, 512),
        (2, 3, 4),
        (2, 2, 4, 1536),
        (2, 2, 4, 512),
        (2, 2, 4),
        (2, 4, 2048),
        (2, 16),
        (2, 16, 512),
        (2, 4),
    )
    return pl.pallas_call(
        write_outputs,
        out_shape=tuple(jax.ShapeDtypeStruct(shape, F32) for shape in shapes),
        in_specs=[whole] * 7,
        out_specs=(whole,) * 10,
        compiler_params=pltpu.CompilerParams(vmem_limit_bytes=60 * 2**20),
    )(*arrays)


def body(
    entry_embeddings,
    norm_scales,
    triple_entry_matrix,
    mixing_exit_matrix,
    exit_bias,
    expanding_matrix,
    former_dense_bias,
    contracting_matrix,
    latter_dense_bias,
    row_presence_indicator,
    problem_column_number,
    loss_gradient,
):
    count = problem_column_number[None]
    results = layers(
        entry_embeddings[0],
        norm_scales,
        triple_entry_matrix,
        mixing_exit_matrix,
        exit_bias,
        expanding_matrix,
        former_dense_bias,
        contracting_matrix,
        latter_dense_bias,
        row_presence_indicator,
        count,
        loss_gradient[0],
    )
    return outputs(*results, count)


def solution(mesh):
    both = ("dp", "fsdp")
    tokens = P("dp", "fsdp", None, None)
    weights = (
        P(None, None, both),
        P(None, None, both, None),
        P(None, None, both, None),
        P(None, None, both),
        P(None, both, None),
        P(None, both),
        P(None, both, None),
        P(None, both),
    )
    return jax.shard_map(
        body,
        mesh=mesh,
        in_specs=(tokens,) + weights + (P("dp", None), P("dp"), tokens),
        out_specs=(tokens, tokens) + weights,
        check_vma=False,
    )
```

```python
import functools

import jax
import jax.numpy as jnp
from jax import lax
from jax.experimental import pallas as pl
from jax.experimental.pallas import tpu as pltpu
from jax.sharding import PartitionSpec as P

EPS = 1e-05
NEG = -1e30
F32 = jnp.float32
BF16 = jnp.bfloat16
MESH = pl.DeviceIdType.MESH
LAYERS = 2
TOK = 256
DIM = 512
VECS = 10
SCALE = 0.125

QKV = (0, 512)
OUT = (384, 896)
INNER = 1024
OUTER = 1536

AG_ORDERS = ("xyz", "yzx", "zxy")
AG_GROUPS = (
    (0, ((0, 128), (128, 256), (256, 384))),
    (0, ((384, 1280), (1280, 1664), (1664, 2048))),
    (1, ((0, 128), (128, 256), (256, 384))),
    (1, ((384, 1280), (1280, 1664), (1664, 2048))),
)
RS_ORDERS = ("zyx", "xzy", "yxz")
RS_GROUPS = (
    ((1024, 1536), (1536, 1792), (1792, 2048)),
    ((384, 768), (768, 896), (896, 1024)),
    ((0, 128), (128, 256), (256, 384)),
)


def dot(a, b):
    return jnp.dot(a, b, preferred_element_type=F32)


def dot_nt(a, b):
    return lax.dot_general(a, b, (((1,), (1,)), ((), ())), preferred_element_type=F32)


def turned(a):
    return a.astype(F32).T.astype(BF16)


def colsum(a):
    return jnp.sum(a, axis=0, keepdims=True)


def lane(shape):
    return lax.broadcasted_iota(jnp.int32, shape, len(shape) - 1)


def kernel(
    entry_ref,
    gains_ref,
    heads_ref,
    merge_ref,
    offs_ref,
    inner_ref,
    thresh_ref,
    outer_ref,
    base_ref,
    present_ref,
    count_ref,
    loss_ref,
    hout_ref,
    gout_ref,
    wout_ref,
    w2out_ref,
    vecout_ref,
    keep_ref,
    G,
    dG,
    recvC,
    R1,
    R2,
    R3,
    fin,
    XB,
    xsend,
    xin,
    xout,
    xfin,
    vsum,
    vrecv,
    VP,
    VB,
    gsum,
    grecv,
    H,
    PK,
    QK,
    PKF,
    MX,
    MXF,
    LSE,
    LSEF,
    osend,
    upsend,
    uprecv,
    dqsend,
    dsend,
    drecv,
    dfeat,
    VALID,
    kmask,
    fmask,
    kh,
    vh,
    tr,
    DK,
    DV,
    A,
    DN,
    ACT,
    DPRE,
    dacc,
    g_ref,
    a2a_s,
    a2a_r,
    ag_s,
    ag_r,
    rs_s,
    rs_r,
    x_s,
    x_r,
    v_s,
    v_r,
):
    dp = lax.axis_index("dp")
    fs = lax.axis_index("fsdp")
    me = {"z": lax.div(dp, 2), "c": lax.rem(dp, 2), "y": lax.div(fs, 4), "x": lax.rem(fs, 4)}

    def device(at):
        return (at["z"] * 2 + at["c"], at["y"] * 4 + at["x"])

    def beside(axis, step):
        at = dict(me)
        at[axis] = lax.rem(me[axis] + step, 2 if axis == "c" else 4)
        return at

    def remote(src, dst, send, recv, at):
        return pltpu.make_async_remote_copy(
            src_ref=src,
            dst_ref=dst,
            send_sem=send,
            recv_sem=recv,
            device_id=device(at),
            device_id_type=MESH,
        )

    barrier = pltpu.get_barrier_semaphore()

    def greet(k, carry):
        at = dict(me)
        at["y"] = lax.rem(me["y"] + lax.div(k, 4), 4)
        at["x"] = lax.rem(me["x"] + lax.rem(k, 4), 4)
        pl.semaphore_signal(barrier, inc=1, device_id=device(at), device_id_type=MESH)
        return carry

    lax.fori_loop(1, 16, greet, 0)
    for step in (1, 2, 3):
        pl.semaphore_signal(barrier, inc=1, device_id=device(beside("z", step)), device_id_type=MESH)
    pl.semaphore_signal(barrier, inc=1, device_id=device(beside("c", 1)), device_id_type=MESH)

    def settle(ref, *sems):
        for sem in sems:
            pltpu.make_async_copy(ref, ref, sem).wait()

    def x_start(n, src, dst):
        for d in (1, 2, 3):
            at = beside("x", d)
            remote(src.at[at["x"]], dst.at[me["x"]], x_s.at[n], x_r.at[n], at).start()
        dst[me["x"]] = src[me["x"]]

    def vec_start(axis, n, buf, recv):
        for d in (1,) if axis == "c" else (1, 2, 3):
            remote(buf, recv.at[n % 4, d - 1], v_s.at[n], v_r.at[n], beside(axis, d)).start()

    def vec_sum(axis, n, buf, recv):
        count = 1 if axis == "c" else 3
        settle(recv.at[n % 4, pl.ds(0, count)], v_s.at[n], v_r.at[n])
        total = buf[...].astype(F32)
        for d in range(count):
            total = total + recv[n % 4, d].astype(F32)
        buf[...] = total.astype(buf.dtype)

    def held(ref, at, cols):
        return ref.at[at["z"], at["c"], at["y"], at["x"], :, pl.ds(cols[0], cols[1] - cols[0])]

    ALL = slice(None)

    def ag_start(group, phase, which=(0, 1, 2)):
        layer, streams = AG_GROUPS[group]
        sems = (ag_s.at[group, phase], ag_r.at[group, phase])
        if phase == 3:
            part = held(
                G.at[layer], dict(z=ALL, c=me["c"], y=ALL, x=ALL), (streams[0][0], streams[2][1])
            )
            remote(part, part, *sems, beside("c", 1)).start()
            return
        for s in which:
            cols, order = streams[s], AG_ORDERS[s]
            at = dict(me)
            for axis in order[:phase]:
                at[axis] = ALL
            part = held(G.at[layer], at, cols)
            for d in (1, 2, 3):
                remote(part, part, *sems, beside(order[phase], d)).start()

    def ag_bytes(group, phase):
        layer, streams = AG_GROUPS[group]
        at = dict(z=pl.ds(0, 3), c=0, y=0, x=0)
        if phase == 3:
            at["z"] = ALL
        if phase >= 1:
            at["y"] = ALL
        if phase >= 2:
            at["x"] = ALL
        return held(G.at[layer], at, (streams[0][0], streams[2][1]))

    def ag_step(group, phase, which=(0, 1, 2)):
        if phase > 0:
            settle(ag_bytes(group, phase - 1), ag_r.at[group, phase - 1])
        if phase < 4:
            ag_start(group, phase, which)

    def plane(k):
        at = dict(me)
        at["y"] = lax.rem(me["y"] + lax.div(k, 4), 4)
        at["x"] = lax.rem(me["x"] + lax.rem(k, 4), 4)
        return at

    def a2a_one(n, k, src, dst):
        at = plane(k)
        return remote(src(at["y"], at["x"]), dst, a2a_s.at[n], a2a_r.at[n], at)

    def a2a_start(n, src, dst):
        def one(k, carry):
            a2a_one(n, k, src, dst).start()
            return carry

        lax.fori_loop(1, 16, one, 0)
        dst[...] = src(me["y"], me["x"])[...]

    def a2a_wait(n, blocks):
        settle(blocks.at[pl.ds(0, 15)], a2a_s.at[n], a2a_r.at[n])

    def a2a_share(n, src, dst, dy, dx):
        k = dy * 4 + dx

        @pl.when(k > 0)
        def _():
            a2a_one(n, k, src, dst).start()

        @pl.when(k == 0)
        def _():
            dst[...] = src(me["y"], me["x"])[...]

    def DG(layer):
        return dG if layer == 1 else G.at[1]

    def vector(layer, j):
        return VB[pl.ds(layer * VECS + j, 1), :]

    def ln_parts(v):
        mean = jnp.mean(v, axis=-1, keepdims=True)
        cen = v - mean
        r = lax.rsqrt(jnp.mean(cen * cen, axis=-1, keepdims=True) + EPS)
        return cen * r, r

    def ln_forward(layer, k):
        gain = vector(layer, k)

        def rows(i, carry):
            at = pl.ds(pl.multiple_of(i * 64, 64), 64)
            hat, unused = ln_parts(H[layer, k, at, :])
            A[layer, k, at, :] = (hat * gain).astype(BF16)
            return carry

        lax.fori_loop(0, 4, rows, 0, unroll=True)

    def ln_backward(layer, k):
        gain = vector(layer, k)

        def rows(i, total):
            at = pl.ds(pl.multiple_of(i * 64, 64), 64)
            hat, r = ln_parts(H[layer, k, at, :])
            dy = dacc[at, :]
            t = dy * gain
            back = r * (
                t
                - jnp.mean(t, axis=-1, keepdims=True)
                - hat * jnp.mean(t * hat, axis=-1, keepdims=True)
            )
            g_ref[at, :] = g_ref[at, :] + back
            return total + colsum(dy * hat)

        put_vector(layer, k, lax.fori_loop(0, 4, rows, jnp.zeros((1, DIM), F32), unroll=True))

    def put_vector(layer, j, row):
        gsum[pl.ds(layer * VECS + j, 1), :] = row

    def weight_cols(layer, g, first, width):
        return G[layer, :, :, :, g, :, first : first + width].reshape(DIM, width)

    def out_matrix(layer, k):
        return jnp.concatenate([weight_cols(layer, g, OUT[k], 128) for g in range(4)], axis=1)

    def project(layer, k, dst, then=None):
        def cols(step, carry):
            g = lax.rem(me["x"] + step, 4)
            out = dot(A[layer, k], weight_cols(layer, g, QKV[k], 384))
            dst[:, g] = out.astype(BF16).reshape(4, 64, 384)
            if then is not None:
                then(step)
            return carry

        lax.fori_loop(0, 4, cols, 0, unroll=True)

    def join(mx):
        return jnp.concatenate([mx[:, p].reshape(TOK, 128) for p in range(4)], axis=1)

    def attention_out(layer, k, mx):
        H[layer, k + 1] = (
            H[layer, k] + dot(join(mx), out_matrix(layer, k)) + vector(layer, 3 + k)
        )

    def head_lanes(shape, h):
        where = lane(shape)
        return (where >= h * 64) & (where < (h + 1) * 64)

    def sample_prepare(layer, backward):
        k = QK[layer, :, :, 128:256].reshape(1024, 128)
        v = QK[layer, :, :, 256:384].reshape(1024, 128)
        where = lane((1024, 128))
        zero = jnp.zeros((1024, 128), BF16)
        for h in range(2):
            mine = head_lanes((1024, 128), h)
            kh[h] = jnp.where(mine, k, jnp.where(where == 64 * (1 - h), kmask[...], zero))
            if backward:
                vh[h] = jnp.where(mine, v, zero)
        tr[...] = turned(k if backward else v)

    def sample_query(layer, i):
        return QK[layer, pl.ds(i * 4, 4), :, 0:128].reshape(256, 128) * jnp.asarray(SCALE, BF16)

    def with_one(q, h):
        return jnp.where(lane((256, 128)) == 64 * (1 - h), jnp.ones((256, 128), BF16), q)

    def sample_forward(layer, then):
        sample_prepare(layer, False)

        def block(step, carry):
            i = lax.rem(me["y"] + step, 4)
            q = sample_query(layer, i)
            parts = []
            for h in range(2):
                s = dot_nt(kh[h], with_one(q, h))
                top = jnp.max(s, axis=0, keepdims=True)
                e = jnp.exp(s - top)
                total = colsum(e)
                LSE[layer, h, i] = top + jnp.log(total)
                parts.append(dot(tr[h * 64 : (h + 1) * 64, :], e.astype(BF16)) / total)
            mixed = jnp.concatenate(parts, axis=0).T.astype(BF16)
            osend[pl.ds(i * 4, 4)] = mixed.reshape(4, 64, 128)
            then(step)
            return carry

        lax.fori_loop(0, 4, block, 0)

    def sample_backward(layer, then):
        sample_prepare(layer, True)

        def block(step, carry):
            i = lax.rem(me["y"] + step, 4)
            q = sample_query(layer, i)
            up = uprecv[layer, pl.ds(i * 4, 4)].reshape(256, 128)
            parts = []
            for h in range(2):
                s = dot_nt(kh[h], with_one(q, h))
                p = jnp.exp(s - LSE[layer, h, i])
                dprobs = dot_nt(vh[h], up)
                t = p * dprobs
                ds = (t - p * colsum(t)).astype(BF16)
                dv = dot(p.astype(BF16), up)
                dk = dot(ds, q)

                @pl.when(step == 0)
                def _():
                    DV[h] = dv
                    DK[h] = dk

                @pl.when(step > 0)
                def _():
                    DV[h] = DV[h] + dv
                    DK[h] = DK[h] + dk

                parts.append(dot(tr[h * 64 : (h + 1) * 64, :], ds))
            dq = (jnp.concatenate(parts, axis=0).T * SCALE).astype(BF16)
            dqsend[pl.ds(i * 4, 4)] = dq.reshape(4, 64, 128)
            then(step)
            return carry

        lax.fori_loop(0, 4, block, 0, unroll=True)
        first = head_lanes((1024, 128), 0)
        dsend[:, :, 0:128] = jnp.where(first, DK[0], DK[1]).astype(BF16).reshape(16, 64, 128)
        dsend[:, :, 128:256] = jnp.where(first, DV[0], DV[1]).astype(BF16).reshape(16, 64, 128)

    def feature_parts(layer, p):
        q = PKF[layer, :, p, :, 0:128].reshape(TOK, 128) * jnp.asarray(SCALE, BF16)
        k = PKF[layer, :, p, :, 128:256].reshape(TOK, 128)
        v = PKF[layer, :, p, :, 256:384].reshape(TOK, 128)
        return q, k, v

    def feature_forward(layer):
        zero = jnp.zeros((TOK, 128), BF16)

        def pair(p, carry):
            q, k, v = feature_parts(layer, p)
            vt = turned(v)
            parts = []
            for h in range(2):
                mine = head_lanes((TOK, 128), h)
                s = dot_nt(jnp.where(mine, k, zero), q) + fmask[...]
                top = jnp.max(s, axis=0, keepdims=True)
                e = jnp.exp(s - top)
                total = colsum(e)
                LSEF[layer, h, p] = top + jnp.log(total)
                parts.append(dot(vt[h * 64 : (h + 1) * 64, :], e.astype(BF16)) / total)
            MXF[layer, :, p] = jnp.concatenate(parts, axis=0).T.astype(BF16).reshape(4, 64, 128)
            return carry

        lax.fori_loop(0, 4, pair, 0, unroll=True)

    def feature_backward(layer):
        zero = jnp.zeros((TOK, 128), BF16)

        def pair(p, carry):
            q, k, v = feature_parts(layer, p)
            up = upsend[:, p].reshape(TOK, 128)
            kt = turned(k)
            dqs, dks, dvs = [], [], []
            for h in range(2):
                mine = head_lanes((TOK, 128), h)
                s = dot_nt(jnp.where(mine, k, zero), q) + fmask[...]
                probs = jnp.exp(s - LSEF[layer, h, p])
                dprobs = dot_nt(jnp.where(mine, v, zero), up)
                t = probs * dprobs
                ds = (t - probs * colsum(t)).astype(BF16)
                dvs.append(dot(probs.astype(BF16), up))
                dks.append(dot(ds, q))
                dqs.append(dot(kt[h * 64 : (h + 1) * 64, :], ds))
            first = head_lanes((TOK, 128), 0)
            dq = (jnp.concatenate(dqs, axis=0).T * SCALE).astype(BF16)
            dfeat[:, p, :, 0:128] = dq.reshape(4, 64, 128)
            dk = jnp.where(first, dks[0], dks[1]).astype(BF16)
            dfeat[:, p, :, 128:256] = dk.reshape(4, 64, 128)
            dv = jnp.where(first, dvs[0], dvs[1]).astype(BF16)
            dfeat[:, p, :, 256:384] = dv.reshape(4, 64, 128)
            return carry

        lax.fori_loop(0, 4, pair, 0, unroll=True)

    def outer_block(layer, g):
        return G[layer, g, :, :, :, :, OUTER : OUTER + 512].reshape(DIM, DIM)

    def gelu_parts(pre):
        inner = 0.7978845608028654 * (pre + 0.044715 * (pre * pre * pre))
        th = jnp.tanh(inner)
        return th

    def ff_forward(layer, last):
        ln_forward(layer, 2)
        dacc[...] = H[layer, 2] + vector(layer, 5)

        def cols(g, carry):
            pre = dot(A[layer, 2], weight_cols(layer, g, INNER, 512)) + vector(layer, 6 + g)
            act = (0.5 * pre * (1.0 + gelu_parts(pre))).astype(BF16)
            dacc[...] = dacc[...] + dot(act, outer_block(layer, g))
            return carry

        lax.fori_loop(0, 4, cols, 0, unroll=True)
        if last:
            hout_ref[...] = dacc[...]
        else:
            H[layer + 1, 0] = dacc[...]

    def round_gradient(layer, j, branch):
        down = g_ref[...].astype(BF16)
        DN[branch] = down
        put_vector(layer, j, colsum(down.astype(F32)))

    def add_up(g, part):
        @pl.when(g == 0)
        def _():
            dacc[...] = part

        @pl.when(g > 0)
        def _():
            dacc[...] = dacc[...] + part

    def ff_backward(layer):
        round_gradient(layer, 5, 2)

        def cols(g, carry):
            w1 = weight_cols(layer, g, INNER, 512)
            pre = dot(A[layer, 2], w1) + vector(layer, 6 + g)
            th = gelu_parts(pre)
            half = 0.5 * (1.0 + th)
            ACT[g] = (pre * half).astype(BF16)
            slope = half + 0.5 * pre * (1.0 - th * th) * (
                0.7978845608028654 * (1.0 + 3 * 0.044715 * (pre * pre))
            )
            dact = dot_nt(DN[2], outer_block(layer, g))
            dpre = (dact * slope).astype(BF16)
            DPRE[g] = dpre
            add_up(g, dot_nt(dpre, w1))
            row = colsum(dpre.astype(F32))
            put_vector(layer, 6 + g, row)
            return carry

        lax.fori_loop(0, 4, cols, 0, unroll=True)
        ln_backward(layer, 2)

    def ff_weights(layer):
        at = turned(A[layer, 2])

        def cols(g, carry):
            DG(layer)[g, :, :, :, :, OUTER : OUTER + 512] = (
                dot(turned(ACT[g]), DN[2]).astype(BF16).reshape(2, 4, 4, 16, 512)
            )
            DG(layer)[:, :, :, g, :, INNER : INNER + 512] = (
                dot(at, DPRE[g]).astype(BF16).reshape(4, 2, 4, 16, 512)
            )
            return carry

        lax.fori_loop(0, 4, cols, 0, unroll=True)

    def attention_out_backward(layer, k):
        round_gradient(layer, 3 + k, k)
        up = dot_nt(DN[k], out_matrix(layer, k)).astype(BF16)
        for p in range(4):
            upsend[:, p] = up[:, p * 128 : (p + 1) * 128].reshape(4, 64, 128)

    def out_weights(layer, k, mx):
        dwo = dot(turned(join(mx)), DN[k]).astype(BF16)
        for g in range(4):
            DG(layer)[:, :, :, g, :, OUT[k] : OUT[k] + 128] = dwo[
                :, g * 128 : (g + 1) * 128
            ].reshape(4, 2, 4, 16, 128)

    def project_backward(layer, k, src):
        def cols(g, carry):
            w = weight_cols(layer, g, QKV[k], 384)
            add_up(g, dot_nt(src[:, g].reshape(TOK, 384), w))
            return carry

        lax.fori_loop(0, 4, cols, 0, unroll=True)
        ln_backward(layer, k)

    def project_weights(layer, k, src):
        at = turned(A[layer, k])

        def cols(g, carry):
            DG(layer)[:, :, :, g, :, QKV[k] : QKV[k] + 384] = (
                dot(at, src[:, g].reshape(TOK, 384)).astype(BF16).reshape(4, 2, 4, 16, 384)
            )
            return carry

        lax.fori_loop(0, 4, cols, 0, unroll=True)

    def rest(order, phase):
        return "".join(a for a in "zyx" if a not in order[:phase])

    def rs_start(layer, group, phase, which=(0, 1, 2)):
        streams = RS_GROUPS[group]
        sems = (rs_s.at[layer * 3 + group, phase], rs_r.at[layer * 3 + group, phase])
        if phase == 0:
            cols = (streams[0][0], streams[2][1])
            src = held(DG(layer), dict(z=ALL, c=beside("c", 1)["c"], y=ALL, x=ALL), cols)
            remote(src, rs_landing(layer, group, 0), *sems, beside("c", 1)).start()
            return
        for s in which:
            cols, order = streams[s], RS_ORDERS[s]
            window = pl.ds(cols[0], cols[1] - cols[0])
            axis = order[phase - 1]
            for d in (1, 2, 3):
                peer = beside(axis, d)
                at = dict(z=ALL, c=me["c"], y=ALL, x=ALL)
                for before in order[: phase - 1]:
                    at[before] = me[before]
                at[axis] = peer[axis]
                if phase == 1:
                    dst = R1.at[d - 1, :, :, :, window]
                elif phase == 2:
                    dst = R2.at[layer, d - 1, :, :, window]
                else:
                    dst = R3.at[layer, d - 1, :, window]
                remote(held(DG(layer), at, cols), dst, *sems, peer).start()

    def rs_landing(layer, group, phase):
        streams = RS_GROUPS[group]
        window = pl.ds(streams[0][0], streams[2][1] - streams[0][0])
        if phase == 0:
            return recvC.at[:, :, :, :, window]
        if phase == 1:
            return R1.at[:, :, :, :, window]
        if phase == 2:
            return R2.at[layer, :, :, :, window]
        return R3.at[layer, :, :, window]

    def rs_sum(layer, group, phase):
        streams = RS_GROUPS[group]
        if phase == 0:
            first, last = streams[0][0], streams[2][1]

            def add(i, carry):
                z, y = lax.div(i, 4), lax.rem(i, 4)
                mine = DG(layer)[z, me["c"], y, :, :, first:last].astype(F32)
                other = recvC[z, y, :, :, first:last].astype(F32)
                DG(layer)[z, me["c"], y, :, :, first:last] = (mine + other).astype(BF16)
                return carry

            lax.fori_loop(0, 16, add, 0)
            return
        for s, (first, last) in enumerate(streams):
            order = RS_ORDERS[s]
            left = rest(order, phase)
            if phase == 1:

                def add(i, carry, left=left, order=order, first=first, last=last):
                    u = lax.div(i, 4)
                    v = lax.rem(i, 4)
                    at = {left[0]: u, left[1]: v, order[0]: me[order[0]]}
                    total = DG(layer)[at["z"], me["c"], at["y"], at["x"], :, first:last].astype(F32)
                    for d in range(3):
                        total = total + R1[d, u, v, :, first:last].astype(F32)
                    DG(layer)[at["z"], me["c"], at["y"], at["x"], :, first:last] = total.astype(BF16)
                    return carry

                lax.fori_loop(0, 16, add, 0)
            elif phase == 2:

                def add(u, carry, left=left, order=order, first=first, last=last):
                    at = dict(me)
                    at[left[0]] = u
                    total = DG(layer)[at["z"], me["c"], at["y"], at["x"], :, first:last].astype(F32)
                    for d in range(3):
                        total = total + R2[layer, d, u, :, first:last].astype(F32)
                    DG(layer)[at["z"], me["c"], at["y"], at["x"], :, first:last] = total.astype(BF16)
                    return carry

                lax.fori_loop(0, 4, add, 0)
            else:
                total = DG(layer)[me["z"], me["c"], me["y"], me["x"], :, first:last].astype(F32)
                for d in range(3):
                    total = total + R3[layer, d, :, first:last].astype(F32)
                fin[layer, :, first:last] = total

    def rs_step(layer, group, phase, which=(0, 1, 2)):
        if phase > 0:
            n = layer * 3 + group
            settle(rs_landing(layer, group, phase - 1), rs_s.at[n, phase - 1], rs_r.at[n, phase - 1])
            rs_sum(layer, group, phase - 1)
        if phase < 4:
            rs_start(layer, group, phase, which)

    for layer in range(LAYERS):
        for g in range(4):

            def cols(ref, at, first, width=128):
                return ref[at + (slice(None), slice(first, first + width))].astype(F32)

            heads = [
                [cols(heads_ref, (layer, k), t * 512 + g * 128) for t in range(3)] for k in range(2)
            ]
            merge = [cols(merge_ref, (layer, k), g * 128) for k in range(2)]
            inner = [cols(inner_ref, (layer,), g * 512 + t * 128) for t in range(4)]
            chunks = heads[0] + merge[:1] + heads[1] + merge[1:] + inner
            for q, chunk in enumerate(chunks):
                kk, gg = q // 3, q % 3
                first = layer * 384 + gg * 128
                XB[g, kk * 4 : kk * 4 + 4, first : first + 128] = chunk
    xsend[...] = XB[...].astype(BF16)

    where = lax.broadcasted_iota(jnp.int32, (1, DIM), 1)
    number = dp * 16 + fs

    def spread(v, width, t):
        out = jnp.zeros((v.shape[0], DIM), F32)
        for r in range(width):
            here = where + t * DIM == number * width + r
            out = jnp.where(here, v[:, r : r + 1], out)
        return out

    VP[...] = jnp.zeros_like(VP)
    gsum[...] = jnp.zeros_like(gsum)
    for layer in range(LAYERS):
        at = layer * VECS
        VP[at : at + 3, :] = spread(gains_ref[layer].astype(F32), 4, 0)
        VP[at + 3 : at + 5, :] = spread(offs_ref[layer].astype(F32), 4, 0)
        VP[at + 5 : at + 6, :] = spread(base_ref[layer : layer + 1, :].astype(F32), 4, 0)
        for t in range(4):
            VP[at + 6 + t : at + 7 + t, :] = spread(
                thresh_ref[layer : layer + 1, :].astype(F32), 16, t
            )
    vsum[...] = VP[...].astype(BF16)
    for layer in range(LAYERS):
        G[layer, me["z"], me["c"], me["y"], me["x"], :, OUTER : OUTER + 512] = outer_ref[layer]
    row = lax.broadcasted_iota(jnp.int32, (64, 64), 0)
    col = lax.broadcasted_iota(jnp.int32, (64, 64), 1)

    def swap_groups(v):
        return (v & 3) | ((v & 12) << 2) | ((v & 48) >> 2)

    perm = jnp.where(swap_groups(row) == col, 1.0, 0.0).astype(BF16)
    VALID[...] = jnp.broadcast_to(present_ref[...].astype(F32), (128, 1024)).T
    kmask[...] = jnp.where(VALID[...] > 0.0, 0.0, NEG).astype(BF16)
    keep_ref[...] = VALID[pl.ds(pl.multiple_of(fs * 64, 64), 64), :]
    key = lax.broadcasted_iota(jnp.int32, (TOK, TOK), 0)
    query = lax.broadcasted_iota(jnp.int32, (TOK, TOK), 1)
    same = ((key & 63) == (query & 63)) & ((key >> 6) < count_ref[...])
    fmask[...] = jnp.where(same, 0.0, NEG)
    pl.semaphore_wait(barrier, 19)
    x_start(0, xsend, xin)
    vec_start("x", 0, vsum, vrecv)
    for f in range(4):
        H[0, 0, f * 64 : (f + 1) * 64, :] = entry_ref[:, f, :].astype(F32)
    settle(xin.at[pl.ds(0, 3)], x_r.at[0])
    mixed_rows = dot(perm, xin[...].reshape(64, 768)).astype(BF16)
    for layer in range(LAYERS):
        for kk in range(4):
            G[layer, me["z"], me["c"], me["y"], me["x"], :, kk * 384 : (kk + 1) * 384] = mixed_rows[
                kk * 16 : (kk + 1) * 16, layer * 384 : (layer + 1) * 384
            ]
    ag_step(0, 0)
    vec_sum("x", 0, vsum, vrecv)
    vec_start("y", 1, vsum, vrecv)
    ag_step(0, 1)
    ag_step(1, 0)
    vec_sum("y", 1, vsum, vrecv)
    vec_start("z", 2, vsum, vrecv)
    ag_step(0, 2)
    ag_step(1, 1)
    vec_sum("z", 2, vsum, vrecv)
    vec_start("c", 3, vsum, vrecv)
    ag_step(0, 3)
    vec_sum("c", 3, vsum, vrecv)
    VB[...] = vsum[...].astype(F32)
    ln_forward(0, 0)
    ag_step(0, 4)

    def fsrc(y, x):
        return PK.at[y, x]

    def osrc(y, x):
        return osend.at[y * 4 + x]

    def usrc(y, x):
        return upsend.at[y, x]

    def dqsrc(y, x):
        return dqsend.at[y * 4 + x]

    def dsrc(y, x):
        return dsend.at[y * 4 + x]

    def to_column(n, src, dst):
        def then(step):
            def one(dy, carry):
                a2a_share(n, src, dst, dy, step)
                return carry

            lax.fori_loop(0, 4, one, 0)

        return then

    def to_row(n, src, dst):
        def then(step):
            def one(dx, carry):
                a2a_share(n, src, dst, step, dx)
                return carry

            lax.fori_loop(0, 4, one, 0)

        return then

    for layer in range(LAYERS):
        if layer > 0:
            ln_forward(layer, 0)
            ag_step(2, 4)
        qdst = QK.at[layer, fs]
        mdst = MX.at[layer, me["y"], me["x"]]
        project(layer, 0, PK, to_column(layer * 5, fsrc, qdst))
        if layer == 0:
            ag_step(1, 2, (0,))
        a2a_wait(layer * 5, QK.at[layer])
        if layer == 0:
            ag_start(1, 2, (1, 2))
            ag_step(2, 0)
            ag_step(3, 0)
        else:
            ag_step(3, 3)
        sample_forward(layer, to_row(layer * 5 + 1, osrc, mdst))
        if layer == 0:
            ag_step(1, 3)
            ag_step(2, 1)
            ag_step(3, 1)
        else:
            ag_step(3, 4)
        a2a_wait(layer * 5 + 1, osend)
        if layer == 0:
            ag_step(1, 4)
        attention_out(layer, 0, MX.at[layer])
        ln_forward(layer, 1)
        project(layer, 1, PKF.at[layer])
        if layer == 0:
            ag_step(2, 2)
            ag_step(3, 2)
        feature_forward(layer)
        attention_out(layer, 1, MXF.at[layer])
        if layer == 0:
            ag_step(2, 3)
        ff_forward(layer, layer == LAYERS - 1)

    for group in range(len(AG_GROUPS)):
        for phase in range(4):
            settle(ag_bytes(group, phase), ag_s.at[group, phase])
    valid = keep_ref[:, 0:1] > 0.0
    for f in range(4):
        real = valid & (count_ref[...] > f)
        g_ref[f * 64 : (f + 1) * 64, :] = jnp.where(real, loss_ref[:, f, :].astype(F32), 0.0)
    for layer in (1, 0):
        udst = uprecv.at[layer, fs]
        dqdst = drecv.at[me["y"], me["x"], :, pl.ds(0, 128)]
        ddst = drecv.at[me["y"], me["x"], :, pl.ds(128, 256)]
        ff_backward(layer)
        ff_weights(layer)
        if layer == 0:
            rs_step(1, 2, 1)
        rs_step(layer, 0, 0)
        if layer == 0:
            rs_step(1, 0, 4)
        attention_out_backward(layer, 1)
        feature_backward(layer)
        if layer == 0:
            rs_step(1, 1, 3)
            rs_step(1, 2, 2)
        project_backward(layer, 1, dfeat)
        attention_out_backward(layer, 0)
        a2a_start(layer * 5 + 2, usrc, udst)
        rs_step(layer, 0, 1, (0,))
        out_weights(layer, 1, MXF.at[layer])
        project_weights(layer, 1, dfeat)
        out_weights(layer, 0, MX.at[layer])
        rs_step(layer, 1, 0)
        if layer == 0:
            rs_step(1, 2, 3)
            rs_step(1, 1, 4)
        a2a_wait(layer * 5 + 2, uprecv.at[layer])
        rs_start(layer, 0, 1, (1, 2))
        sample_backward(layer, to_row(layer * 5 + 3, dqsrc, dqdst))
        a2a_start(layer * 5 + 4, dsrc, ddst)
        rs_step(layer, 0, 2)
        rs_step(layer, 1, 1, (0,))
        if layer == 0:
            rs_step(1, 2, 4)
        a2a_wait(layer * 5 + 3, dqsend)
        a2a_wait(layer * 5 + 4, dsend)
        rs_start(layer, 1, 1, (1, 2))
        project_weights(layer, 0, drecv)
        rs_step(layer, 2, 0)
        project_backward(layer, 0, drecv)
        rs_step(layer, 0, 3)
        rs_step(layer, 1, 2)
    gout_ref[...] = g_ref[...]

    vec_start("x", 4, gsum, grecv)
    rs_step(0, 2, 1)
    rs_step(0, 0, 4)
    vec_sum("x", 4, gsum, grecv)
    vec_start("y", 5, gsum, grecv)
    rs_step(0, 1, 3)
    rs_step(0, 2, 2)
    vec_sum("y", 5, gsum, grecv)
    vec_start("z", 6, gsum, grecv)
    rs_step(0, 1, 4)
    rs_step(0, 2, 3)
    vec_sum("z", 6, gsum, grecv)
    vec_start("c", 7, gsum, grecv)
    rs_step(0, 2, 4)
    w2out_ref[...] = fin[:, :, OUTER : OUTER + 512]
    stacked = jnp.concatenate(
        [
            jnp.concatenate([fin[l, :, kk * 384 : (kk + 1) * 384] for l in range(LAYERS)], axis=1)
            for kk in range(4)
        ],
        axis=0,
    ).astype(BF16)
    xout[...] = dot(perm, stacked).astype(BF16).reshape(4, 16, 768)
    x_start(1, xout, xfin)
    vec_sum("c", 7, gsum, grecv)
    at = lax.broadcasted_iota(jnp.int32, (DIM, 128), 0)
    to = lax.broadcasted_iota(jnp.int32, (DIM, 128), 1)
    exact = lax.Precision.HIGHEST
    few = jnp.where((at == number * 4 + to) & (to < 4), 1.0, 0.0)
    many = jnp.where((at == lax.rem(number, 32) * 16 + to) & (to < 16), 1.0, 0.0)
    few = jnp.dot(gsum[...], few, precision=exact, preferred_element_type=F32)
    many = jnp.dot(gsum[...], many, precision=exact, preferred_element_type=F32)
    vecout_ref[0:24, :] = few
    for layer in range(LAYERS):
        first = layer * VECS + 6
        line = jnp.zeros((1, 128), F32)
        for t in range(4):
            line = line + jnp.where(lax.div(number, 32) == t, many[first + t : first + t + 1], 0.0)
        vecout_ref[24 + layer : 25 + layer, :] = line
    settle(xfin.at[pl.ds(0, 3)], x_s.at[1], x_r.at[1])
    wout_ref[...] = xfin[...].astype(F32)
    settle(xin.at[pl.ds(0, 3)], x_s.at[0])


def write_outputs(
    h_ref,
    g_ref,
    w_ref,
    w2_ref,
    vec_ref,
    keep_ref,
    count_ref,
    act_out,
    tokens_out,
    gains_out,
    heads_out,
    merge_out,
    offs_out,
    inner_out,
    thresh_out,
    outer_out,
    base_out,
):
    valid = keep_ref[:, 0:1] > 0.0
    for f in range(4):
        rows = slice(f * 64, (f + 1) * 64)
        act_out[0, :, f, :] = jnp.where(valid & (count_ref[...] > f), h_ref[rows, :], 0.0)
        tokens_out[0, :, f, :] = g_ref[rows, :]
    for layer in range(LAYERS):
        for g in range(4):
            for q in range(12):
                kk, gg = q // 3, q % 3
                first = layer * 384 + gg * 128
                chunk = w_ref[g, kk * 4 : kk * 4 + 4, first : first + 128]
                if q in (3, 7):
                    merge_out[layer, q // 4, :, g * 128 : (g + 1) * 128] = chunk
                elif q < 8:
                    to = (q % 4) * 512 + g * 128
                    heads_out[layer, q // 4, :, to : to + 128] = chunk
                else:
                    to = g * 512 + (q - 8) * 128
                    inner_out[layer, :, to : to + 128] = chunk
        at = layer * VECS
        gains_out[layer] = vec_ref[at : at + 3, 0:4]
        offs_out[layer] = vec_ref[at + 3 : at + 5, 0:4]
        base_out[layer : layer + 1, :] = vec_ref[at + 5 : at + 6, 0:4]
        thresh_out[layer : layer + 1, :] = vec_ref[24 + layer : 25 + layer, 0:16]
    outer_out[...] = w2_ref[...]


def vmem(shape, dtype):
    return pltpu.VMEM(shape, dtype)


def layers(*arrays):
    dma = pltpu.SemaphoreType.DMA
    whole = pl.BlockSpec(memory_space=pltpu.VMEM)
    return pl.pallas_call(
        kernel,
        out_shape=(
            jax.ShapeDtypeStruct((TOK, DIM), F32),
            jax.ShapeDtypeStruct((TOK, DIM), F32),
            jax.ShapeDtypeStruct((4, 16, 768), F32),
            jax.ShapeDtypeStruct((LAYERS, 16, 512), F32),
            jax.ShapeDtypeStruct((32, 128), F32),
            jax.ShapeDtypeStruct((64, 128), F32),
        ),
        in_specs=[whole] * 12,
        out_specs=(whole,) * 6,
        scratch_shapes=[
            vmem((2, 4, 2, 4, 4, 16, 2048), BF16),
            vmem((4, 2, 4, 4, 16, 2048), BF16),
            vmem((4, 4, 4, 16, 2048), BF16),
            vmem((3, 4, 4, 16, 2048), BF16),
            vmem((2, 3, 4, 16, 2048), BF16),
            vmem((2, 3, 16, 2048), BF16),
            vmem((2, 16, 2048), F32),
            vmem((4, 16, 768), F32),
            vmem((4, 16, 768), BF16),
            vmem((4, 16, 768), BF16),
            vmem((4, 16, 768), BF16),
            vmem((4, 16, 768), BF16),
            vmem((32, 512), BF16),
            vmem((4, 3, 32, 512), BF16),
            vmem((32, 512), F32),
            vmem((32, 512), F32),
            vmem((24, 512), F32),
            vmem((4, 3, 24, 512), F32),
            vmem((2, 3, TOK, DIM), F32),
            vmem((4, 4, 64, 384), BF16),
            vmem((2, 16, 64, 384), BF16),
            vmem((2, 4, 4, 64, 384), BF16),
            vmem((2, 4, 4, 64, 128), BF16),
            vmem((2, 4, 4, 64, 128), BF16),
            vmem((2, 2, 4, 1, 256), F32),
            vmem((2, 2, 4, 1, 256), F32),
            vmem((16, 64, 128), BF16),
            vmem((4, 4, 64, 128), BF16),
            vmem((2, 16, 64, 128), BF16),
            vmem((16, 64, 128), BF16),
            vmem((16, 64, 256), BF16),
            vmem((4, 4, 64, 384), BF16),
            vmem((4, 4, 64, 384), BF16),
            vmem((1024, 128), F32),
            vmem((1024, 128), BF16),
            vmem((TOK, TOK), F32),
            vmem((2, 1024, 128), BF16),
            vmem((2, 1024, 128), BF16),
            vmem((128, 1024), BF16),
            vmem((2, 1024, 128), F32),
            vmem((2, 1024, 128), F32),
            vmem((2, 3, TOK, DIM), BF16),
            vmem((3, TOK, DIM), BF16),
            vmem((4, TOK, DIM), BF16),
            vmem((4, TOK, DIM), BF16),
            vmem((TOK, DIM), F32),
            vmem((TOK, DIM), F32),
            dma((10,)),
            dma((10,)),
            dma((4, 4)),
            dma((4, 4)),
            dma((6, 4)),
            dma((6, 4)),
            dma((2,)),
            dma((2,)),
            dma((8,)),
            dma((8,)),
        ],
        compiler_params=pltpu.CompilerParams(
            collective_id=0, has_side_effects=True, vmem_limit_bytes=63 * 2**20
        ),
    )(*arrays)


def outputs(*arrays):
    whole = pl.BlockSpec(memory_space=pltpu.VMEM)
    shapes = (
        (1, 64, 4, 512),
        (1, 64, 4, 512),
        (2, 3, 4),
        (2, 2, 4, 1536),
        (2, 2, 4, 512),
        (2, 2, 4),
        (2, 4, 2048),
        (2, 16),
        (2, 16, 512),
        (2, 4),
    )
    return pl.pallas_call(
        write_outputs,
        out_shape=tuple(jax.ShapeDtypeStruct(shape, F32) for shape in shapes),
        in_specs=[whole] * 7,
        out_specs=(whole,) * 10,
        compiler_params=pltpu.CompilerParams(vmem_limit_bytes=60 * 2**20),
    )(*arrays)


def body(
    entry_embeddings,
    norm_scales,
    triple_entry_matrix,
    mixing_exit_matrix,
    exit_bias,
    expanding_matrix,
    former_dense_bias,
    contracting_matrix,
    latter_dense_bias,
    row_presence_indicator,
    problem_column_number,
    loss_gradient,
):
    count = problem_column_number[None]
    results = layers(
        entry_embeddings[0],
        norm_scales,
        triple_entry_matrix,
        mixing_exit_matrix,
        exit_bias,
        expanding_matrix,
        former_dense_bias,
        contracting_matrix,
        latter_dense_bias,
        row_presence_indicator,
        count,
        loss_gradient[0],
    )
    return outputs(*results, count)


def solution(mesh):
    both = ("dp", "fsdp")
    tokens = P("dp", "fsdp", None, None)
    weights = (
        P(None, None, both),
        P(None, None, both, None),
        P(None, None, both, None),
        P(None, None, both),
        P(None, both, None),
        P(None, both),
        P(None, both, None),
        P(None, both),
    )
    return jax.shard_map(
        body,
        mesh=mesh,
        in_specs=(tokens,) + weights + (P("dp", None), P("dp"), tokens),
        out_specs=(tokens, tokens) + weights,
        check_vma=False,
    )
```
